512 devices in a mesh: row: 32 (over z, core), col: 16 (over y, x).
Axes of the slice: x: 4, y: 4, z: 16, core: 2. Of those that a mesh axis runs over, the one named last changes fastest.
Arguments:
- inverse_root: float32 [32, 16, 2, 384, 192], P('row', 'col'), may hold values from -0.0546875 to 0.0546875
- inverse_upper: float32 [32, 16, 2, 192, 192], P('row', 'col'), may hold values from -0.078125 to 0.078125
- inverse_middle: float32 [32, 16, 2, 384, 192], P('row', 'col'), may hold values from -0.078125 to 0.078125
- inverse_lower: float32 [32, 16, 2, 192, 192], P('row', 'col'), may hold values from -0.109375 to 0.109375
- leaf_inverse: float32 [32, 16, 2, 384, 384], P('row', 'col'), may hold values from -0.21875 to 0.21875
- source_root: float32 [32, 1, 192, 128], P('row'), may hold values from -6 to 6
- source_upper: float32 [32, 1, 192, 128], P('row'), may hold values from -6 to 6
- source_middle: float32 [32, 2, 192, 128], P('row'), may hold values from -6 to 6
- source_lower: float32 [32, 2, 192, 128], P('row'), may hold values from -6 to 6
- leaf_source: float32 [32, 16, 384, 128], P('row', 'col'), may hold values from -6 to 6
- update_root: float32 [32, 1, 2, 2, 96, 32], P('row'), may hold values from -0.75 to 0.75
- update_upper: float32 [32, 1, 2, 2, 96, 32], P('row'), may hold values from -0.75 to 0.75
- update_middle: float32 [32, 2, 2, 2, 96, 32], P('row'), may hold values from -0.75 to 0.75
- leaf_update: float32 [32, 16, 2, 96, 32], P('row', 'col'), may hold values from -0.75 to 0.75
- slots_root: int32 [32, 1, 2, 96], P('row'), may hold values from 0 to 192, as said below
- slots_upper: int32 [32, 1, 2, 96], P('row'), may hold values from 0 to 192, as said below
- slots_middle: int32 [32, 2, 2, 96], P('row'), may hold values from 0 to 192, as said below
- leaf_slots: int32 [32, 16, 96], P('row', 'col'), may hold values from 0 to 192, as said below
- basis_upper: float32 [16, 2, 2, 192, 32], P('col'), may hold values from -0.078125 to 0.078125
- basis_middle: float32 [16, 2, 2, 384, 32], P('col'), may hold values from -0.078125 to 0.078125
- basis_lower: float32 [16, 4, 2, 192, 32], P('col'), may hold values from -0.109375 to 0.109375
- leaf_basis: float32 [32, 16, 2, 384, 32], P('row', 'col'), may hold values from -0.21875 to 0.21875
- front_ranks: int32 [14], replicated, may hold values from 8 to 32, as said below
- leaf_ranks: int32 [32, 16], P('row', 'col'), may hold values from 8 to 32, as said below
Outputs:
- solution_root: float32 [32, 16, 12, 128], P('row', 'col')
- solution_upper: float32 [32, 16, 12, 128], P('row', 'col')
- solution_middle: float32 [32, 16, 24, 128], P('row', 'col')
- solution_lower: float32 [32, 16, 24, 128], P('row', 'col')
- leaf_solution: float32 [32, 16, 384, 128], P('row', 'col')
The draws below stay inside these ranges and needn't reach their ends.
Inputs may be any that keep to these rules, and one draw needn't show every extreme that they name: `slots_root`: within one row of slots the entries below 192 are distinct; 192 marks an unused slot; every row of slots has at least half of its slots used and at least one unused. `slots_upper`: as for slots_root. `slots_middle`: as for slots_root. `leaf_slots`: as for slots_root. `front_ranks`: some front has rank 32. `leaf_ranks`: some subtree has rank 32.
All inputs are finite; a program needn't handle non-finite values.
Results may differ from the reference program's by a relative error of at most 0.00013.
Values sent between devices are 32-bit elements; how exact they have to be, the bound alone decides.
No kernel may reach another device: no remote copies, remote signals or barrier semaphores. Data moves between devices by JAX's collectives and lax.ppermute only.
A program may use at most 64 MiB of HBM per device.

```python
import jax
import jax.numpy as jnp
from jax import lax

SEPARATOR = 192
LEAF_ROWS = 384
MAX_RANK = 32
SOURCES = 64
UPDATE_SLOTS = 96
FRONT_ROOT = 6144
FRONT_UPPER = 3072
FRONT_LOWER = 1536
BLOCK_ROOT = 384
BLOCK_UPPER = 192
BLOCK_MIDDLE = 384
BLOCK_LOWER = 192
N_ROW = 32
N_COL = 16


def slot_rows(key, count):

    def one_row(row_key):
        pick_key, live_key, order_key = jax.random.split(row_key, 3)
        chosen = jax.random.permutation(pick_key, SEPARATOR)[:UPDATE_SLOTS]
        live_count = jax.random.randint(live_key, (), UPDATE_SLOTS // 2, UPDATE_SLOTS)
        slot_order = jax.random.permutation(order_key, UPDATE_SLOTS)
        return jnp.where(slot_order < live_count, chosen, SEPARATOR).astype(jnp.int32)
    return jax.vmap(one_row)(jax.random.split(key, count))


def rank_table(key, count):
    table_key, spot_key = jax.random.split(key)
    rank_draw = jax.random.randint(table_key, (count,), MAX_RANK // 4, MAX_RANK + 1)
    full_spot = jax.random.randint(spot_key, (), 0, count)
    return jnp.where(jnp.arange(count) == full_spot, MAX_RANK, rank_draw).astype(jnp.int32)


def draw_slots_root(key, part):
    return slot_rows(jax.random.fold_in(key, 11), N_ROW * 2).reshape(N_ROW, 1, 2, UPDATE_SLOTS)


def draw_slots_upper(key, part):
    return slot_rows(jax.random.fold_in(key, 12), N_ROW * 2).reshape(N_ROW, 1, 2, UPDATE_SLOTS)


def draw_slots_middle(key, part):
    return slot_rows(jax.random.fold_in(key, 13), N_ROW * 4).reshape(N_ROW, 2, 2, UPDATE_SLOTS)


def draw_leaf_slots(key, part):
    return slot_rows(jax.random.fold_in(key, 14), N_ROW * N_COL).reshape(N_ROW, N_COL, UPDATE_SLOTS)


def draw_front_ranks(key, part):
    return rank_table(jax.random.fold_in(key, 21), 14)


def draw_leaf_ranks(key, part):
    return rank_table(jax.random.fold_in(key, 22), N_ROW * N_COL).reshape(N_ROW, N_COL)


def steps_of(own_key, dims, cuts, low, largest):
    gain = 1.0
    for axis_at, blocks in cuts:
        steps = jax.random.uniform(jax.random.fold_in(jax.random.fold_in(own_key, 6), axis_at), (blocks,), jnp.float32, low / len(cuts), largest / len(cuts))
        gain = gain * jnp.repeat(jnp.exp(steps), dims[axis_at] // blocks).reshape((-1,) + (1,) * (len(dims) - 1 - axis_at))
    return gain


def noise(key, dims, scale, reach, shards=(), kind=jnp.bfloat16):
    array = scale * jax.random.normal(key, dims, jnp.float32)
    if shards:
        array = array * steps_of(key, dims, shards, -0.22, 0.18)
    return jnp.clip(array, -reach, reach).astype(kind)


def setup_inputs(seed: int = 0) -> dict:
    splits = jax.random.split(jax.random.key(seed), 25)
    inverse_root = noise(splits[0], (N_ROW, N_COL, 2, BLOCK_ROOT, SEPARATOR), (2 * FRONT_ROOT) ** -0.5, 0.0546875, ((0, 32), (1, 16)), jnp.float32)
    inverse_upper = noise(splits[1], (N_ROW, N_COL, 2, BLOCK_UPPER, SEPARATOR), (2 * FRONT_UPPER) ** -0.5, 0.078125, ((0, 32), (1, 16)), jnp.float32)
    inverse_middle = noise(splits[2], (N_ROW, N_COL, 2, BLOCK_MIDDLE, SEPARATOR), (2 * FRONT_UPPER) ** -0.5, 0.078125, ((0, 32), (1, 16)), jnp.float32)
    inverse_lower = noise(splits[3], (N_ROW, N_COL, 2, BLOCK_LOWER, SEPARATOR), (2 * FRONT_LOWER) ** -0.5, 0.109375, ((0, 32), (1, 16)), jnp.float32)
    leaf_inverse = noise(splits[4], (N_ROW, N_COL, 2, LEAF_ROWS, LEAF_ROWS), (2 * LEAF_ROWS) ** -0.5, 0.21875, ((0, 32), (1, 16)), jnp.float32)
    source_root = noise(splits[5], (N_ROW, 1, SEPARATOR, 2 * SOURCES), 1.0, 6.0, ((0, 32),), jnp.float32)
    source_upper = noise(splits[6], (N_ROW, 1, SEPARATOR, 2 * SOURCES), 1.0, 6.0, ((0, 32),), jnp.float32)
    source_middle = noise(splits[7], (N_ROW, 2, SEPARATOR, 2 * SOURCES), 1.0, 6.0, ((0, 32),), jnp.float32)
    source_lower = noise(splits[8], (N_ROW, 2, SEPARATOR, 2 * SOURCES), 1.0, 6.0, ((0, 32),), jnp.float32)
    leaf_source = noise(splits[9], (N_ROW, N_COL, LEAF_ROWS, 2 * SOURCES), 1.0, 6.0, ((0, 32), (1, 16)), jnp.float32)
    update_root = noise(splits[10], (N_ROW, 1, 2, 2, UPDATE_SLOTS, MAX_RANK), (2 * MAX_RANK) ** -0.5, 0.75, ((0, 32),), jnp.float32)
    update_upper = noise(splits[11], (N_ROW, 1, 2, 2, UPDATE_SLOTS, MAX_RANK), (2 * MAX_RANK) ** -0.5, 0.75, ((0, 32),), jnp.float32)
    update_middle = noise(splits[12], (N_ROW, 2, 2, 2, UPDATE_SLOTS, MAX_RANK), (2 * MAX_RANK) ** -0.5, 0.75, ((0, 32),), jnp.float32)
    leaf_update = noise(splits[13], (N_ROW, N_COL, 2, UPDATE_SLOTS, MAX_RANK), (2 * MAX_RANK) ** -0.5, 0.75, ((0, 32), (1, 16)), jnp.float32)
    slots_root = draw_slots_root(jax.random.fold_in(splits[24], 71), 0)
    slots_upper = draw_slots_upper(jax.random.fold_in(splits[24], 71), 0)
    slots_middle = draw_slots_middle(jax.random.fold_in(splits[24], 71), 0)
    leaf_slots = draw_leaf_slots(jax.random.fold_in(splits[24], 71), 0)
    basis_upper = noise(splits[18], (N_COL, 2, 2, BLOCK_UPPER, MAX_RANK), (2 * FRONT_UPPER) ** -0.5, 0.078125, ((0, 16),), jnp.float32)
    basis_middle = noise(splits[19], (N_COL, 2, 2, BLOCK_MIDDLE, MAX_RANK), (2 * FRONT_UPPER) ** -0.5, 0.078125, ((0, 16),), jnp.float32)
    basis_lower = noise(splits[20], (N_COL, 4, 2, BLOCK_LOWER, MAX_RANK), (2 * FRONT_LOWER) ** -0.5, 0.109375, ((0, 16),), jnp.float32)
    leaf_basis = noise(splits[21], (N_ROW, N_COL, 2, LEAF_ROWS, MAX_RANK), (2 * LEAF_ROWS) ** -0.5, 0.21875, ((0, 32), (1, 16)), jnp.float32)
    front_ranks = draw_front_ranks(jax.random.fold_in(splits[24], 71), 0)
    leaf_ranks = draw_leaf_ranks(jax.random.fold_in(splits[24], 71), 0)
    return {"inverse_root": inverse_root, "inverse_upper": inverse_upper, "inverse_middle": inverse_middle, "inverse_lower": inverse_lower, "leaf_inverse": leaf_inverse, "source_root": source_root, "source_upper": source_upper, "source_middle": source_middle, "source_lower": source_lower, "leaf_source": leaf_source, "update_root": update_root, "update_upper": update_upper, "update_middle": update_middle, "leaf_update": leaf_update, "slots_root": slots_root, "slots_upper": slots_upper, "slots_middle": slots_middle, "leaf_slots": leaf_slots, "basis_upper": basis_upper, "basis_middle": basis_middle, "basis_lower": basis_lower, "leaf_basis": leaf_basis, "front_ranks": front_ranks, "leaf_ranks": leaf_ranks}


precise = lax.Precision.HIGHEST


def combine(stacked):
    half_width = stacked.shape[-1] // 2
    real_part = stacked[..., 0, :, :]
    imag_part = stacked[..., 1, :, :]
    return jnp.concatenate([real_part[..., :half_width] - imag_part[..., half_width:], real_part[..., half_width:] + imag_part[..., :half_width]], axis=-1)


def product(matrix, vector):
    return combine(jnp.einsum("...zmk,...kc->...zmc", matrix, vector, precision=precise))


def product_back(matrix, vector):
    return combine(jnp.einsum("...zkm,...kc->...zmc", matrix, vector, precision=precise))


def spread(row_index, values, height):
    return jnp.zeros((height, values.shape[-1]), values.dtype).at[row_index].add(values, mode="drop")


def pick_rows(source_block, row_index):
    padded = jnp.concatenate([source_block, jnp.zeros((1, source_block.shape[-1]), source_block.dtype)], axis=0)
    return jnp.take(padded, row_index, axis=0)


def masked(values, rank_limit):
    keep_rows = jnp.arange(values.shape[-2])[:, None] < rank_limit[..., None, None]
    return jnp.where(keep_rows, values, jnp.zeros_like(values))


def reference(inverse_root, inverse_upper, inverse_middle, inverse_lower, leaf_inverse, source_root, source_upper, source_middle, source_lower, leaf_source, update_root, update_upper, update_middle, leaf_update, slots_root, slots_upper, slots_middle, leaf_slots, basis_upper, basis_middle, basis_lower, leaf_basis, front_ranks, leaf_ranks):
    grid_rows = (N_ROW, N_ROW // 2, N_ROW // 2, N_ROW // 4)
    grid_cols = (N_COL, N_COL, N_COL // 2, N_COL // 2)
    row_groups = (1, 2, 2, 4)
    col_groups = (1, 1, 2, 2)
    rank_base = (0, 0, 2, 6)
    inverses = (inverse_root, inverse_upper, inverse_middle, inverse_lower)
    right_sides = (source_root, source_upper, source_middle, source_lower)
    updates = (update_root, update_upper, update_middle)
    slot_maps = (slots_root, slots_upper, slots_middle)
    basis_sets = (None, basis_upper, basis_middle, basis_lower)
    width = 2 * SOURCES

    def ranks_of(height):
        count = row_groups[height] * col_groups[height]
        return front_ranks[rank_base[height]:rank_base[height] + count].reshape(row_groups[height], col_groups[height])

    def tile_view(height):
        tiles = inverses[height]
        return tiles.reshape((row_groups[height], grid_rows[height], col_groups[height], grid_cols[height]) + tiles.shape[2:])

    def basis_view(height):
        basis = basis_sets[height]
        return basis.reshape((col_groups[height], grid_cols[height]) + basis.shape[1:])

    def solve_level(height, right_side):
        blocks = right_side.reshape(row_groups[height], grid_rows[height], col_groups[height], SEPARATOR, width)
        return combine(jnp.einsum("xiyjzba,xiyac->xyjzbc", tile_view(height), blocks, precision=precise))

    def back_level(height, vector):
        stacked = jnp.einsum("xiyjzba,xyjbc->xiyzac", tile_view(height), vector, precision=precise)
        return combine(stacked).reshape(N_ROW, col_groups[height], SEPARATOR, width)

    def weights_of(height, forward):
        stacked = jnp.einsum("yjxzbr,xyjbc->xyzrc", basis_view(height), forward, precision=precise)
        return masked(combine(stacked), ranks_of(height))

    def expand(height, coeffs):
        return combine(jnp.einsum("yjxzbr,xyrc->xyjzbc", basis_view(height), coeffs, precision=precise))

    def pair_up(height, weights_now):
        if height == 1:
            return jnp.transpose(weights_now, (1, 0, 2, 3))[None]
        if height == 2:
            return weights_now[:, None]
        return jnp.transpose(weights_now.reshape(2, 2, 2, MAX_RANK, width), (0, 2, 1, 3, 4))

    def split_up(height, summed):
        if height == 1:
            return jnp.transpose(summed[0], (1, 0, 2, 3))
        if height == 2:
            return summed[:, 0]
        return jnp.transpose(summed, (0, 2, 1, 3, 4)).reshape(4, 2, MAX_RANK, width)

    def contributions(parent, pairs):
        per_row = jnp.repeat(pairs, grid_rows[parent], axis=0)
        terms = product(updates[parent], per_row)
        scatter_one = lambda row_index, values: spread(row_index, values, SEPARATOR)
        scattered = jax.vmap(jax.vmap(jax.vmap(scatter_one)))(slot_maps[parent], terms)
        return scattered[:, :, 0] + scattered[:, :, 1]

    def tile_rows(source_block, index_rows):
        return jax.vmap(lambda one_index: pick_rows(source_block, one_index))(index_rows)

    def gathered(parent, solved):
        rows_taken = jax.vmap(jax.vmap(tile_rows))(solved, slot_maps[parent])
        partials = product_back(updates[parent], rows_taken)
        return partials.reshape(row_groups[parent], grid_rows[parent], col_groups[parent], 2, MAX_RANK, width).sum(axis=1)

    leaf_forward = product(leaf_inverse, leaf_source)
    leaf_coeffs = masked(product_back(leaf_basis, leaf_forward), leaf_ranks)
    leaf_terms = product(leaf_update, leaf_coeffs)
    scatter_leaf = lambda row_index, values: spread(row_index, values, SEPARATOR)
    leaf_spread = jax.vmap(jax.vmap(scatter_leaf))(leaf_slots, leaf_terms)
    right_side = source_lower - leaf_spread.reshape(N_ROW, 2, grid_cols[3], SEPARATOR, width).sum(axis=2)
    forwards = [None, None, None, None]
    for height in (3, 2, 1, 0):
        forward = solve_level(height, right_side)
        forwards[height] = forward
        if height > 0:
            weights_now = weights_of(height, forward)
            right_side = right_sides[height - 1] - contributions(height - 1, pair_up(height, weights_now))
    solved = back_level(0, forwards[0])
    backwards = [solved]
    for height in (1, 2, 3):
        coeffs = masked(split_up(height, gathered(height - 1, solved)), ranks_of(height))
        residual = forwards[height] - expand(height, coeffs)
        solved = back_level(height, residual)
        backwards.append(solved)
    lower_tiles = jnp.repeat(backwards[3], grid_cols[3], axis=1)
    leaf_rows = jax.vmap(jax.vmap(pick_rows))(lower_tiles, leaf_slots)
    leaf_back_coeffs = masked(product_back(leaf_update, leaf_rows), leaf_ranks)
    leaf_back = leaf_forward - product(leaf_basis, leaf_back_coeffs)
    leaf_solution = product_back(leaf_inverse, leaf_back)
    results = [backwards[height].reshape(N_ROW, N_COL, SEPARATOR // grid_cols[height], width) for height in range(4)]
    return (results[0], results[1], results[2], results[3], leaf_solution)
```

```python
import jax
import jax.numpy as jnp
from jax import lax
from jax.sharding import Mesh, PartitionSpec as P

precise = lax.Precision.HIGHEST

ROW = ("a", "e", "z", "k")
COL = ("d", "c")
CHIPS = ("a", "e", "z")
PLANE = ("k", "d", "c")


def exchange(pieces, axes):
    return lax.all_to_all(pieces, axes, 0, 0)


def share(values, axes, count):
    return exchange(jnp.broadcast_to(values[None], (count,) + values.shape), axes)


def combine(stacked):
    half = stacked.shape[-1] // 2
    real, imag = stacked[..., 0, :, :], stacked[..., 1, :, :]
    return jnp.concatenate(
        [real[..., :half] - imag[..., half:], real[..., half:] + imag[..., :half]], axis=-1
    )


def product(matrix, vector):
    return combine(jnp.einsum("...zmk,...kc->...zmc", matrix, vector, precision=precise))


def product_back(matrix, vector):
    return combine(jnp.einsum("...zkm,...kc->...zmc", matrix, vector, precision=precise))


def product_pair(matrix, left, right):
    stacked = jnp.einsum(
        "zmk,kc->zmc", matrix, jnp.concatenate([left, right], axis=-1), precision=precise
    )
    width = left.shape[-1]
    return combine(stacked[..., :width]), combine(stacked[..., width:])


def product_back_pair(matrix, left, right):
    stacked = jnp.einsum(
        "zkm,kc->zmc", matrix, jnp.concatenate([left, right], axis=-1), precision=precise
    )
    width = left.shape[-1]
    return combine(stacked[..., :width]), combine(stacked[..., width:])


def as_matrix(values):
    half = values.shape[-1] // 2
    return jnp.stack([values[..., :half], values[..., half:]], axis=-3)


def masked(values, rank_limit):
    keep = jnp.arange(values.shape[-2])[:, None] < jnp.asarray(rank_limit)[..., None, None]
    return jnp.where(keep, values, jnp.zeros_like(values))


def select(array, position):
    return lax.dynamic_index_in_dim(array, position, 0, keepdims=False)


def spread(slots, update, height):
    onehot = (jnp.arange(height)[None, :, None] == slots[:, None, :]).astype(jnp.float32)
    flat = jnp.concatenate([update[:, 0], update[:, 1]], axis=-1)
    return jnp.einsum("nhm,nmr->nhr", onehot, flat, precision=precise)


def body(
    inverse_root,
    inverse_upper,
    inverse_middle,
    inverse_lower,
    leaf_inverse,
    source_root,
    source_upper,
    source_middle,
    source_lower,
    leaf_source,
    update_root,
    update_upper,
    update_middle,
    leaf_update,
    slots_root,
    slots_upper,
    slots_middle,
    leaf_slots,
    basis_upper,
    basis_middle,
    basis_lower,
    leaf_basis,
    front_ranks,
    leaf_ranks,
):
    a, e, k, d = (lax.axis_index(name) for name in ("a", "e", "k", "d"))
    inverses = (inverse_root[0, 0], inverse_upper[0, 0], inverse_middle[0, 0], inverse_lower[0, 0])
    sources = (
        source_root[0, 0],
        source_upper[0, 0],
        select(source_middle[0], d),
        select(source_lower[0], d),
    )
    basis1 = select(basis_upper[0], a)
    basis2 = select(basis_middle[0], a)
    basis3 = select(basis_lower[0], 2 * a + e)
    rank1 = front_ranks[0:2]
    rank2 = front_ranks[2:6].reshape(2, 2)
    rank3 = front_ranks[6:14].reshape(2, 2, 2)
    leaf_rank = leaf_ranks[0, 0]
    separator, width = sources[0].shape
    half = width // 2

    all_slots = jnp.concatenate(
        [slots_root[0, 0], slots_upper[0, 0], select(slots_middle[0], d), leaf_slots[0]], axis=0
    )
    all_updates = jnp.concatenate(
        [update_root[0, 0], update_upper[0, 0], select(update_middle[0], d), leaf_update[0]], axis=0
    )
    spreads = spread(all_slots, all_updates, separator)
    rank = spreads.shape[-1] // 2
    children = [
        jnp.concatenate(
            [
                spreads[2 * h, :, :rank],
                spreads[2 * h + 1, :, :rank],
                spreads[2 * h, :, rank:],
                spreads[2 * h + 1, :, rank:],
            ],
            axis=-1,
        )
        for h in range(3)
    ]

    leaf_forward = product(leaf_inverse[0, 0], leaf_source[0, 0])
    leaf_coeffs = masked(product_back(leaf_basis[0, 0], leaf_forward), leaf_rank)
    own_spread = spreads[6]
    packed = jnp.concatenate([own_spread[: separator // 2], own_spread[separator // 2 :]], axis=-1)
    shared = share(jnp.concatenate([leaf_coeffs, packed], axis=0), ("c",), 8)
    others = shared[:, :rank]
    packs = shared[:, rank:]
    leaf_maps = jnp.concatenate([packs[..., :half], packs[..., half:]], axis=1)
    leaf_maps = jnp.stack([leaf_maps[..., :rank], leaf_maps[..., rank:]], axis=1)
    side_lower = sources[3] - product(leaf_maps, others).sum(axis=0)
    partial3 = product(inverses[3], side_lower)

    applied = [product_pair(inverses[h], sources[h], children[h]) for h in range(3)]
    low3 = product_back(basis3, partial3)
    low2 = product_back_pair(basis2, *applied[2])
    low1 = product_back_pair(basis1, *applied[1])

    rows = jnp.stack([low3, low2[0], low2[1], low1[0], low1[1]], axis=1)
    rows = exchange(rows, PLANE).reshape(2, 2, 8, 5, width).sum(axis=(0, 2))
    rows = jnp.concatenate(
        [rows[:, 0], rows[:, 1], rows[:, 2], (rows[0, 3:] + rows[1, 3:])], axis=0
    )
    got = share(rows, CHIPS, 16).reshape(2, 2, 4, 8, width).sum(axis=2)
    merged = got.sum(axis=1)
    rows = jnp.concatenate(
        [
            got[:, :, 0:2].reshape(8, width),
            merged[:, 2:4].reshape(4, width),
            merged[:, 4:6].reshape(4, width),
            merged[:, 6],
            merged[:, 7],
            jnp.zeros((4, width), jnp.float32),
        ],
        axis=0,
    )
    blocks = jnp.transpose(share(rows, PLANE, 32), (1, 0, 2))
    coeffs3 = masked(blocks[0:8].reshape(2, 2, 2, rank, width), rank3)
    total2 = blocks[8:12].reshape(2, 2, rank, width)
    gain2 = as_matrix(blocks[12:16].reshape(2, 2, rank, width))
    total1 = blocks[16:18]
    gain1 = as_matrix(blocks[18:20])
    pairs3 = jnp.transpose(coeffs3, (0, 2, 1, 3, 4)).reshape(2, 2, 2 * rank, width)
    coeffs2 = masked(total2 - product(gain2, pairs3), rank2)
    pairs2 = coeffs2.reshape(2, 2 * rank, width)
    coeffs1 = masked(total1 - product(gain1, pairs2), rank1)
    below = (coeffs1.reshape(2 * rank, width), select(pairs2, a), select(select(pairs3, a), d))

    maps = [as_matrix(applied[h][1]) for h in range(3)]
    partials = [applied[h][0] - product(maps[h], below[h]) for h in range(3)] + [partial3]
    pad = jnp.zeros((2, separator // 6, width), jnp.float32)
    halves = [p.reshape(2, p.shape[0] // 2, width) for p in partials]
    wide = jnp.concatenate([halves[0], halves[2]], axis=1).reshape(2, 16, 24, width)
    thin = jnp.concatenate([halves[1], pad, halves[3], pad], axis=1).reshape(2, 16, 16, width)
    pieces = jnp.concatenate([wide, thin], axis=2)
    pieces = exchange(pieces, ("k",)).sum(axis=0)
    sums = exchange(pieces, CHIPS).reshape(2, 2, 4, 40, width).sum(axis=2)
    upper_sums = jnp.broadcast_to(sums.sum(axis=1, keepdims=True), sums.shape)
    root_sums = jnp.broadcast_to(sums.sum(axis=(0, 1), keepdims=True), sums.shape)
    first = a == 0
    pieces = jnp.concatenate(
        [
            jnp.where(first, root_sums[:, :, :24], upper_sums[:, :, :24]),
            jnp.where(first, upper_sums[:, :, 24:], sums[:, :, 24:]),
        ],
        axis=2,
    )
    pieces = jnp.broadcast_to(pieces[:, :, None], (2, 2, 4, 40, width)).reshape(16, 40, width)
    pieces = exchange(pieces, CHIPS)
    mine = jnp.concatenate(
        [
            pieces[:8, :24].reshape(separator, width),
            pieces[8:, :24].reshape(separator, width),
            pieces[:8, 24:].reshape(128, width)[: separator // 2],
            pieces[8:, 24:].reshape(128, width)[: separator // 2],
        ],
        axis=0,
    )
    both = share(mine, ("k",), 2)
    half_rows = separator // 2
    forwards = (
        both[:, :separator].reshape(2 * separator, width),
        both[:, 2 * separator : 2 * separator + half_rows].reshape(separator, width),
        both[:, separator : 2 * separator].reshape(2 * separator, width),
        both[:, 2 * separator + half_rows :].reshape(separator, width),
    )

    lows = [product_back(maps[h], forwards[h]).reshape(2, rank, width) for h in range(3)]
    rows = jnp.transpose(jnp.concatenate(lows, axis=0), (1, 0, 2))
    rows = exchange(rows, PLANE).reshape(2, 2, 8, 6, width).sum(axis=(0, 2))
    joined = rows[0, :4] + rows[1, :4]
    pieces = jnp.stack(
        [
            jnp.stack(
                [
                    jnp.concatenate(
                        [
                            joined[to_a : to_a + 1],
                            joined[2:4],
                            rows[:, 4 + to_e],
                            jnp.zeros((3, width), jnp.float32),
                        ],
                        axis=0,
                    )
                    for to_e in range(2)
                ]
            )
            for to_a in range(2)
        ]
    )
    pieces = jnp.broadcast_to(pieces[:, :, None], (2, 2, 4, 8, width)).reshape(16, 8, width)
    got = exchange(pieces, CHIPS).reshape(2, 8, 8, width).sum(axis=1)
    near = select(got, a)
    root_row = got[0, 0:1] + got[1, 0:1]
    pieces = jnp.stack(
        [
            jnp.concatenate(
                [root_row, near[1 + to_d : 2 + to_d], near[3 + to_d : 4 + to_d], root_row], axis=0
            )
            for to_d in range(2)
        ]
    )
    pieces = jnp.broadcast_to(pieces[None, :, None], (2, 2, 8, 4, width)).reshape(32, 4, width)
    blocks = jnp.transpose(exchange(pieces, PLANE), (1, 0, 2))
    back1 = masked(blocks[0], select(rank1, a))
    gain1_own = select(gain1, a).reshape(2, rank, 2, rank)
    gain1_own = lax.dynamic_index_in_dim(gain1_own, d, 2, keepdims=False)
    back2 = masked(
        blocks[1] - product_back(gain1_own, back1), select(select(rank2, a), d)
    )
    gain2_own = select(select(gain2, a), d).reshape(2, rank, 2, rank)
    gain2_own = lax.dynamic_index_in_dim(gain2_own, e, 2, keepdims=False)
    back3 = masked(
        blocks[2] - product_back(gain2_own, back2), select(select(select(rank3, a), e), d)
    )

    residuals = (
        forwards[0],
        forwards[1] - product(basis1, back1),
        forwards[2] - product(basis2, back2),
        forwards[3] - product(basis3, back3),
    )
    solved = [product_back(inverses[h], residuals[h]) for h in range(4)]
    leaf_parts = product_back(leaf_maps, jnp.broadcast_to(solved[3][None], (8,) + solved[3].shape))
    tops = [jnp.transpose(solved[h].reshape(2, 8, 12, width), (1, 0, 2, 3)) for h in range(2)]
    tops = jnp.stack(tops, axis=2).reshape(8, 48, width)
    pieces = jnp.concatenate(
        [tops, solved[2].reshape(8, 24, width), solved[3].reshape(8, 24, width), leaf_parts], axis=1
    )
    total = exchange(pieces, ("c",)).sum(axis=0)
    tops = total[:48].reshape(2, 24, width)
    tops = select(tops, d) + lax.ppermute(select(tops, 1 - d), "d", [(0, 1), (1, 0)])
    leaf_back_coeffs = masked(total[96:], leaf_rank)
    leaf_back = leaf_forward - product(leaf_basis[0, 0], leaf_back_coeffs)
    leaf_solution = product_back(leaf_inverse[0, 0], leaf_back)
    return (
        tops[None, None, :12],
        tops[None, None, 12:],
        total[None, None, 48:72],
        total[None, None, 72:96],
        leaf_solution[None, None],
    )


def solution(mesh):
    fine = Mesh(mesh.devices.reshape(2, 2, 4, 2, 2, 8), ROW + COL)
    tile = (ROW, COL)
    in_specs = (
        [P(*tile, None, None, None)] * 5
        + [P(ROW, None, None, None)] * 4
        + [P(*tile, None, None)]
        + [P(ROW, None, None, None, None, None)] * 3
        + [P(*tile, None, None, None)]
        + [P(ROW, None, None, None)] * 3
        + [P(*tile, None)]
        + [P(COL, None, None, None, None)] * 3
        + [P(*tile, None, None, None), P(), P(*tile)]
    )
    return jax.shard_map(
        body,
        mesh=fine,
        in_specs=tuple(in_specs),
        out_specs=(P(*tile, None, None),) * 5,
        check_vma=False,
    )
```

```python
import jax
import jax.numpy as jnp
from jax import lax
from jax.sharding import Mesh, PartitionSpec as P

precise = lax.Precision.HIGHEST

ROW = ("a", "e", "z", "k")
COL = ("d", "c")
CHIPS = ("a", "e", "z")
PLANE = ("k", "d", "c")


def exchange(pieces, axes):
    return lax.all_to_all(pieces, axes, 0, 0)


def share(values, axes, count):
    return exchange(jnp.broadcast_to(values[None], (count,) + values.shape), axes)


def partner(values, axis):
    return lax.ppermute(values, axis, [(0, 1), (1, 0)])


def fold(halves, place):
    return select(halves, place) + partner(select(halves, 1 - place), "k")


def combine(stacked):
    half = stacked.shape[-1] // 2
    real, imag = stacked[..., 0, :, :], stacked[..., 1, :, :]
    return jnp.concatenate(
        [real[..., :half] - imag[..., half:], real[..., half:] + imag[..., :half]], axis=-1
    )


def product(matrix, vector):
    return combine(jnp.einsum("...zmk,...kc->...zmc", matrix, vector, precision=precise))


def product_back(matrix, vector):
    return combine(jnp.einsum("...zkm,...kc->...zmc", matrix, vector, precision=precise))


def product_pair(matrix, left, right):
    stacked = jnp.einsum(
        "zmk,kc->zmc", matrix, jnp.concatenate([left, right], axis=-1), precision=precise
    )
    width = left.shape[-1]
    return combine(stacked[..., :width]), combine(stacked[..., width:])


def product_back_pair(matrix, left, right):
    stacked = jnp.einsum(
        "zkm,kc->zmc", matrix, jnp.concatenate([left, right], axis=-1), precision=precise
    )
    width = left.shape[-1]
    return combine(stacked[..., :width]), combine(stacked[..., width:])


def as_matrix(values):
    half = values.shape[-1] // 2
    return jnp.stack([values[..., :half], values[..., half:]], axis=-3)


def masked(values, rank_limit):
    keep = jnp.arange(values.shape[-2])[:, None] < jnp.asarray(rank_limit)[..., None, None]
    return jnp.where(keep, values, jnp.zeros_like(values))


def select(array, position):
    return lax.dynamic_index_in_dim(array, position, 0, keepdims=False)


def spread(slots, update, height):
    onehot = (jnp.arange(height)[None, :, None] == slots[:, None, :]).astype(jnp.float32)
    flat = jnp.concatenate([update[:, 0], update[:, 1]], axis=-1)
    return jnp.einsum("nhm,nmr->nhr", onehot, flat, precision=precise)


def body(
    inverse_root,
    inverse_upper,
    inverse_middle,
    inverse_lower,
    leaf_inverse,
    source_root,
    source_upper,
    source_middle,
    source_lower,
    leaf_source,
    update_root,
    update_upper,
    update_middle,
    leaf_update,
    slots_root,
    slots_upper,
    slots_middle,
    leaf_slots,
    basis_upper,
    basis_middle,
    basis_lower,
    leaf_basis,
    front_ranks,
    leaf_ranks,
):
    a, e, k, d = (lax.axis_index(name) for name in ("a", "e", "k", "d"))
    inverses = (inverse_root[0, 0], inverse_upper[0, 0], inverse_middle[0, 0], inverse_lower[0, 0])
    sources = (
        source_root[0, 0],
        source_upper[0, 0],
        select(source_middle[0], d),
        select(source_lower[0], d),
    )
    basis1 = select(basis_upper[0], a)
    basis2 = select(basis_middle[0], a)
    basis3 = select(basis_lower[0], 2 * a + e)
    rank1 = front_ranks[0:2]
    rank2 = front_ranks[2:6].reshape(2, 2)
    rank3 = front_ranks[6:14].reshape(2, 2, 2)
    leaf_rank = leaf_ranks[0, 0]
    separator, width = sources[0].shape
    half = width // 2

    all_slots = jnp.concatenate(
        [slots_root[0, 0], slots_upper[0, 0], select(slots_middle[0], d), leaf_slots[0]], axis=0
    )
    all_updates = jnp.concatenate(
        [update_root[0, 0], update_upper[0, 0], select(update_middle[0], d), leaf_update[0]], axis=0
    )
    spreads = spread(all_slots, all_updates, separator)
    rank = spreads.shape[-1] // 2
    children = [
        jnp.concatenate(
            [
                spreads[2 * h, :, :rank],
                spreads[2 * h + 1, :, :rank],
                spreads[2 * h, :, rank:],
                spreads[2 * h + 1, :, rank:],
            ],
            axis=-1,
        )
        for h in range(3)
    ]

    applied = [product_pair(inverses[h], sources[h], children[h]) for h in range(3)]
    pad = jnp.zeros((2, separator // 6, width), jnp.float32)
    parts = []
    for side in range(2):
        first_half = [applied[h][side].reshape(2, -1, width) for h in range(3)]
        wide = jnp.concatenate([first_half[0], first_half[2]], axis=1)
        thin = jnp.concatenate([first_half[1], pad], axis=1)
        parts += [wide.reshape(2, 16, 24, width), thin.reshape(2, 16, 8, width)]
    pieces = jnp.concatenate([parts[0], parts[2], parts[1], parts[3]], axis=2)
    applied_pieces = fold(pieces, k)

    leaf_forward = product(leaf_inverse[0, 0], leaf_source[0, 0])
    leaf_coeffs = masked(product_back(leaf_basis[0, 0], leaf_forward), leaf_rank)
    own_spread = spreads[6]
    packed = jnp.concatenate([own_spread[: separator // 2], own_spread[separator // 2 :]], axis=-1)
    shared = share(jnp.concatenate([leaf_coeffs, packed], axis=0), ("c",), 8)
    others = shared[:, :rank]
    packs = shared[:, rank:]
    leaf_maps = jnp.concatenate([packs[..., :half], packs[..., half:]], axis=1)
    leaf_maps = jnp.stack([leaf_maps[..., :rank], leaf_maps[..., rank:]], axis=1)
    side_lower = sources[3] - product(leaf_maps, others).sum(axis=0)
    partial3 = product(inverses[3], side_lower)

    low3 = product_back(basis3, partial3)
    low2 = product_back_pair(basis2, *applied[2])
    low1 = product_back_pair(basis1, *applied[1])
    thin = jnp.concatenate([partial3.reshape(2, -1, width), pad], axis=1)
    lower_pieces = fold(thin.reshape(2, 16, 8, width), k)

    rows = jnp.stack([low3, low2[0], low2[1], low1[0], low1[1]], axis=1)
    rows = exchange(rows, PLANE).reshape(2, 2, 8, 5, width).sum(axis=(0, 2))
    rows = jnp.concatenate(
        [rows[:, 0], rows[:, 1], rows[:, 2], (rows[0, 3:] + rows[1, 3:])], axis=0
    )
    pieces = jnp.concatenate(
        [jnp.broadcast_to(rows[None], (16, 8, width)), lower_pieces, applied_pieces], axis=1
    )
    slices = exchange(pieces, CHIPS).reshape(2, 2, 4, 80, width).sum(axis=2)
    sums = slices[:, :, 16:].sum(axis=1)
    got = slices[:, :, :16]
    lower_slices = got[:, :, 8:]
    merged = got.sum(axis=1)
    rows = jnp.concatenate(
        [
            got[:, :, 0:2].reshape(8, width),
            merged[:, 2:4].reshape(4, width),
            merged[:, 4:6].reshape(4, width),
            merged[:, 6],
            merged[:, 7],
            jnp.zeros((4, width), jnp.float32),
        ],
        axis=0,
    )
    blocks = jnp.transpose(share(rows, PLANE, 32), (1, 0, 2))
    coeffs3 = masked(blocks[0:8].reshape(2, 2, 2, rank, width), rank3)
    total2 = blocks[8:12].reshape(2, 2, rank, width)
    gain2 = as_matrix(blocks[12:16].reshape(2, 2, rank, width))
    total1 = blocks[16:18]
    gain1 = as_matrix(blocks[18:20])
    pairs3 = jnp.transpose(coeffs3, (0, 2, 1, 3, 4)).reshape(2, 2, 2 * rank, width)
    coeffs2 = masked(total2 - product(gain2, pairs3), rank2)
    pairs2 = coeffs2.reshape(2, 2 * rank, width)
    coeffs1 = masked(total1 - product(gain1, pairs2), rank1)
    pair1 = coeffs1.reshape(2 * rank, width)

    first = a == 0
    wide = jnp.where(first, jnp.broadcast_to(sums.sum(axis=0), sums.shape), sums)[:, :48]
    wide_below = jnp.where(
        first, pair1[None], lax.dynamic_index_in_dim(pairs3, d, 1, keepdims=False)
    )
    wide_map = as_matrix(wide[:, 24:])
    wide_forward = wide[:, :24] - product(wide_map, wide_below)
    upper_map = as_matrix(sums[:, 56:])
    upper_forward = sums[:, 48:56] - product(upper_map, pairs2)

    wide_low = product_back(wide_map, wide_forward).reshape(4, rank, width)
    upper_low = product_back(upper_map, upper_forward).reshape(4, rank, width)
    rows = jnp.transpose(jnp.concatenate([wide_low, upper_low], axis=0), (1, 0, 2))
    rows = exchange(rows, PLANE).reshape(2, 2, 8, 8, width).sum(axis=(0, 2))
    joined = rows[0] + rows[1]
    nothing = jnp.zeros((1, width), jnp.float32)
    tail = jnp.zeros((4, width), jnp.float32)
    pieces = jnp.stack(
        [
            jnp.stack(
                [
                    jnp.concatenate(
                        [
                            wide_forward[to_a],
                            upper_forward[to_a],
                            lower_slices[to_a, to_e],
                            jnp.where(
                                first,
                                jnp.concatenate([joined[to_a : to_a + 1], nothing], axis=0),
                                rows[:, 2 * to_a + to_e],
                            ),
                            joined[4 + 2 * to_a : 6 + 2 * to_a],
                            tail,
                        ],
                        axis=0,
                    )
                    for to_e in range(2)
                ]
            )
            for to_a in range(2)
        ]
    )
    pieces = jnp.broadcast_to(pieces[:, :, None], (2, 2, 4, 48, width)).reshape(16, 48, width)
    got = exchange(pieces, CHIPS)
    half_rows = separator // 2
    mine = jnp.concatenate(
        [
            got[:8, :24].reshape(separator, width),
            got[8:, :24].reshape(separator, width),
            got[:, 24:32].reshape(128, width)[:half_rows],
            got[:, 32:40].reshape(128, width)[:half_rows],
        ],
        axis=0,
    )
    theirs = partner(mine, "k")
    both = jnp.stack([jnp.where(k == 0, mine, theirs), jnp.where(k == 0, theirs, mine)])
    forwards = (
        both[:, :separator].reshape(2 * separator, width),
        both[:, 2 * separator : 2 * separator + half_rows].reshape(separator, width),
        both[:, separator : 2 * separator].reshape(2 * separator, width),
        both[:, 2 * separator + half_rows :].reshape(separator, width),
    )
    lows = got[:, 40:44].reshape(2, 8, 4, width).sum(axis=1)
    upper_rows = lows[0, 2:] + lows[1, 2:]
    pieces = jnp.stack(
        [
            jnp.concatenate(
                [lows[0, :1], upper_rows[to_d : to_d + 1], lows[1, to_d : to_d + 1], nothing],
                axis=0,
            )
            for to_d in range(2)
        ]
    )
    pieces = jnp.broadcast_to(pieces[None, :, None], (2, 2, 8, 4, width)).reshape(32, 4, width)
    blocks = jnp.transpose(exchange(pieces, PLANE), (1, 0, 2))
    back1 = masked(blocks[0], select(rank1, a))
    gain1_own = select(gain1, a).reshape(2, rank, 2, rank)
    gain1_own = lax.dynamic_index_in_dim(gain1_own, d, 2, keepdims=False)
    back2 = masked(
        blocks[1] - product_back(gain1_own, back1), select(select(rank2, a), d)
    )
    gain2_own = select(select(gain2, a), d).reshape(2, rank, 2, rank)
    gain2_own = lax.dynamic_index_in_dim(gain2_own, e, 2, keepdims=False)
    back3 = masked(
        blocks[2] - product_back(gain2_own, back2), select(select(select(rank3, a), e), d)
    )

    residuals = (
        forwards[0],
        forwards[1] - product(basis1, back1),
        forwards[2] - product(basis2, back2),
        forwards[3] - product(basis3, back3),
    )
    solved = [product_back(inverses[h], residuals[h]) for h in range(4)]
    leaf_parts = product_back(leaf_maps, jnp.broadcast_to(solved[3][None], (8,) + solved[3].shape))
    tops = [jnp.transpose(solved[h].reshape(2, 8, 12, width), (1, 0, 2, 3)) for h in range(2)]
    tops = jnp.stack(tops, axis=2).reshape(8, 48, width)
    pieces = jnp.concatenate(
        [tops, solved[2].reshape(8, 24, width), solved[3].reshape(8, 24, width), leaf_parts], axis=1
    )
    total = exchange(pieces, ("c",)).sum(axis=0)
    tops = total[:48].reshape(2, 24, width)
    tops = select(tops, d) + partner(select(tops, 1 - d), "d")
    leaf_back_coeffs = masked(total[96:], leaf_rank)
    leaf_back = leaf_forward - product(leaf_basis[0, 0], leaf_back_coeffs)
    leaf_solution = product_back(leaf_inverse[0, 0], leaf_back)
    return (
        tops[None, None, :12],
        tops[None, None, 12:],
        total[None, None, 48:72],
        total[None, None, 72:96],
        leaf_solution[None, None],
    )


def solution(mesh):
    fine = Mesh(mesh.devices.reshape(2, 2, 4, 2, 2, 8), ROW + COL)
    tile = (ROW, COL)
    in_specs = (
        [P(*tile, None, None, None)] * 5
        + [P(ROW, None, None, None)] * 4
        + [P(*tile, None, None)]
        + [P(ROW, None, None, None, None, None)] * 3
        + [P(*tile, None, None, None)]
        + [P(ROW, None, None, None)] * 3
        + [P(*tile, None)]
        + [P(COL, None, None, None, None)] * 3
        + [P(*tile, None, None, None), P(), P(*tile)]
    )
    return jax.shard_map(
        body,
        mesh=fine,
        in_specs=tuple(in_specs),
        out_specs=(P(*tile, None, None),) * 5,
        check_vma=False,
    )
```

```python
import jax
import jax.numpy as jnp
from jax import lax
from jax.experimental import pallas as pl
from jax.experimental.pallas import tpu as pltpu
from jax.sharding import Mesh, PartitionSpec as P

precise = lax.Precision.HIGHEST

ROW = ("a", "e", "z", "k")
COL = ("d", "c")
CHIPS = ("a", "e", "z")
PLANE = ("k", "d", "c")


def exchange(pieces, axes):
    return lax.all_to_all(pieces, axes, 0, 0)


def share(values, axes, count):
    return exchange(jnp.broadcast_to(values[None], (count,) + values.shape), axes)


def partner(values, axis):
    return lax.ppermute(values, axis, [(0, 1), (1, 0)])


def combine(stacked):
    half = stacked.shape[-1] // 2
    real, imag = stacked[..., 0, :, :], stacked[..., 1, :, :]
    return jnp.concatenate(
        [real[..., :half] - imag[..., half:], real[..., half:] + imag[..., :half]], axis=-1
    )


def product(matrix, vector):
    return combine(jnp.einsum("...zmk,...kc->...zmc", matrix, vector, precision=precise))


def product_back(matrix, vector):
    return combine(jnp.einsum("...zkm,...kc->...zmc", matrix, vector, precision=precise))


def turned(values):
    groups = []
    for at in range(0, values.shape[-1], 128):
        groups += [-values[:, at + 64 : at + 128], values[:, at : at + 64]]
    return jnp.concatenate(groups, axis=-1)


def dot(left, right, contract=1):
    return lax.dot_general(
        left,
        right,
        (((contract,), (0,)), ((), ())),
        precision=precise,
        preferred_element_type=jnp.float32,
    )


def times(real, imag, vector):
    return dot(real, vector) + dot(imag, turned(vector))


def times_back(real, imag, vector):
    return dot(real, vector, 0) + dot(imag, turned(vector), 0)


def cut(values, limit):
    rows = lax.broadcasted_iota(jnp.int32, values.shape, 0)
    return jnp.where(rows < limit, values, jnp.zeros_like(values))


def leaf_kernel(ranks, inverse, source, basis, update, slots, forward, packs):
    inner = inverse.shape[-1]
    result = times(inverse[0, 0, 0], inverse[0, 0, 1], source[0, 0])
    forward[...] = result
    low = cut(times_back(basis[0, 0, 0], basis[0, 0, 1], result), ranks[0, 0])
    height = inner // 2
    places = lax.broadcasted_iota(jnp.int32, (height, slots.shape[-1]), 0)
    onehot = (places == slots[0]).astype(jnp.float32)
    flat = jnp.concatenate([update[0, 0, 0], update[0, 0, 1]], axis=-1)
    spread_out = lax.dot_general(
        flat,
        onehot,
        (((0,), (1,)), ((), ())),
        precision=precise,
        preferred_element_type=jnp.float32,
    )
    half = low.shape[0]
    pack = jnp.concatenate(
        [
            low,
            spread_out[:, :128],
            jnp.concatenate([spread_out[:half, 128:], spread_out[half:, 128:]], axis=-1),
        ],
        axis=0,
    )
    for place in range(packs.shape[0]):
        packs[place] = pack


def apply_kernel(
    spots,
    inverse0,
    inverse1,
    inverse2,
    source0,
    source1,
    source2,
    update0,
    update1,
    update2,
    slots0,
    slots1,
    slots2,
    basis1,
    basis2,
    keep,
    send,
    lows,
):
    a, k, d = spots[0], spots[2], spots[3]
    results = []
    for inverse, source, update, slots, at in (
        (inverse0, source0, update0, slots0, 0),
        (inverse1, source1, update1, slots1, 0),
        (inverse2, source2, update2, slots2, d),
    ):
        right = source[0, at]
        height = right.shape[0]
        lists = slots[0, at]
        places = lax.broadcasted_iota(jnp.int32, (height, lists.shape[-1]), 0)
        spread_out = []
        for child in range(2):
            onehot = (places == lists[child : child + 1]).astype(jnp.float32)
            flat = jnp.concatenate([update[0, at, child, 0], update[0, at, child, 1]], axis=-1)
            spread_out.append(dot(onehot, flat))
        rank = spread_out[0].shape[-1] // 2
        both = jnp.concatenate(
            [
                right,
                spread_out[0][:, :rank],
                spread_out[1][:, :rank],
                spread_out[0][:, rank:],
                spread_out[1][:, rank:],
            ],
            axis=-1,
        )
        results.append(times(inverse[0, 0, 0], inverse[0, 0, 1], both))
    low2 = times_back(basis2[0, a, 0], basis2[0, a, 1], results[2])
    low1 = times_back(basis1[0, a, 0], basis1[0, a, 1], results[1])
    lows[0] = low2[:, :128]
    lows[1] = low2[:, 128:]
    lows[2] = low1[:, :128]
    lows[3] = low1[:, 128:]

    def put(target, half):
        for side in range(2):
            for level, at in ((0, 0), (2, 8)):
                rows = results[level].shape[0] // 2
                part = results[level][half * rows : (half + 1) * rows, side * 128 : side * 128 + 128]
                target[at : at + 8, 24 * side : 24 * side + 24] = part.reshape(8, 24, 128)
            rows = results[1].shape[0] // 2
            part = results[1][half * rows : (half + 1) * rows, side * 128 : side * 128 + 128]
            row = 48 + 8 * side
            target[0:12, row : row + 8] = part.reshape(12, 8, 128)
            target[12:16, row : row + 8] = jnp.zeros((4, 8, 128), jnp.float32)

    for half in range(2):

        @pl.when(k == half)
        def _(half=half):
            put(keep, half)
            put(send, 1 - half)


def lower_kernel(spots, shared, inverse, source, basis, lows, keep, send, rows):
    a, e, k, d = spots[0], spots[1], spots[2], spots[3]
    low = shared[:, 0:32].reshape(256, 128)
    low_turned = turned(low)
    packs = shared[:, 96:128].reshape(256, 128)
    top = dot(shared[:, 32:64].reshape(256, 128), low, 0) + dot(
        shared[:, 64:96].reshape(256, 128), low_turned, 0
    )
    rest = dot(packs[:, :64], low, 0) + dot(packs[:, 64:], low_turned, 0)
    side = source[0, d] - jnp.concatenate([top, rest], axis=0)
    partial = times(inverse[0, 0, 0], inverse[0, 0, 1], side)
    front = 2 * a + e
    low3 = times_back(basis[0, front, 0], basis[0, front, 1], partial)
    rows[:, 0, :] = low3
    for at in range(4):
        rows[:, at + 1, :] = lows[at]
    for at in range(5, 8):
        rows[:, at, :] = jnp.zeros((32, 128), jnp.float32)
    count = partial.shape[0] // 2

    def put(target, half):
        target[0:12] = partial[half * count : (half + 1) * count].reshape(12, 8, 128)
        target[12:16] = jnp.zeros((4, 8, 128), jnp.float32)

    for half in range(2):

        @pl.when(k == half)
        def _(half=half):
            put(keep, half)
            put(send, 1 - half)


def backward_kernel(
    spots,
    ranks,
    gains,
    lows,
    mine,
    theirs,
    inverse0,
    inverse1,
    inverse2,
    inverse3,
    basis1,
    basis2,
    basis3,
    shared,
    pieces,
):
    a, e, k, d = spots[0], spots[1], spots[2], spots[3]

    def gain_back(gain, low, child):
        both = times_back(gain[:, :64], gain[:, 64:], low)
        return jnp.where(child == 0, both[:32], both[32:])

    gain1 = jnp.where(a == 0, gains[:, 18, :], gains[:, 19, :])
    gain2 = jnp.where(
        a == 0,
        jnp.where(d == 0, gains[:, 12, :], gains[:, 13, :]),
        jnp.where(d == 0, gains[:, 14, :], gains[:, 15, :]),
    )
    back1 = cut(lows[:, 0, :], ranks[a])
    back2 = cut(lows[:, 1, :] - gain_back(gain1, back1, d), ranks[2 + 2 * a + d])
    back3 = cut(lows[:, 2, :] - gain_back(gain2, back2, e), ranks[6 + 4 * a + 2 * e + d])

    def whole(start, stop):
        left, right = mine[start:stop], theirs[start:stop]
        return jnp.concatenate(
            [jnp.where(k == 0, left, right), jnp.where(k == 0, right, left)], axis=0
        )

    front = 2 * a + e
    residuals = (
        whole(0, 192),
        whole(384, 480) - times(basis1[0, a, 0], basis1[0, a, 1], back1),
        whole(192, 384) - times(basis2[0, a, 0], basis2[0, a, 1], back2),
        whole(480, 576) - times(basis3[0, front, 0], basis3[0, front, 1], back3),
    )
    solved = [
        times_back(inverse[0, 0, 0], inverse[0, 0, 1], residuals[level])
        for level, inverse in enumerate((inverse0, inverse1, inverse2, inverse3))
    ]
    for level in range(2):
        for place in range(2):
            for to_c in range(8):
                at = 96 * place + 12 * to_c
                row = 24 * place + 12 * level
                pieces[to_c, row : row + 12] = solved[level][at : at + 12]
    pieces[:, 48:72] = solved[2].reshape(8, 24, 128)
    pieces[:, 72:96] = solved[3].reshape(8, 24, 128)
    lowest = solved[3]
    lowest_turned = turned(lowest)
    packs = shared[:, 96:128].reshape(256, 128)
    parts = (
        dot(shared[:, 32:64].reshape(256, 128), lowest[:128])
        + dot(shared[:, 64:96].reshape(256, 128), lowest_turned[:128])
        + dot(packs[:, :64], lowest[128:])
        + dot(packs[:, 64:], lowest_turned[128:])
    )
    pieces[:, 96:128] = parts.reshape(8, 32, 128)


def last_kernel(ranks, low, forward, inverse, basis, solved):
    back = cut(low[...], ranks[0, 0])
    rest = forward[...] - times(basis[0, 0, 0], basis[0, 0, 1], back)
    solved[0, 0] = times_back(inverse[0, 0, 0], inverse[0, 0, 1], rest)


def call(kernel, shapes, scalars, arrays, flops):
    return pl.pallas_call(
        kernel,
        out_shape=[jax.ShapeDtypeStruct(shape, jnp.float32) for shape in shapes],
        in_specs=[pl.BlockSpec(memory_space=pltpu.SMEM)] * len(scalars)
        + [pl.BlockSpec(memory_space=pltpu.VMEM)] * len(arrays),
        out_specs=[pl.BlockSpec(memory_space=pltpu.VMEM)] * len(shapes),
        compiler_params=pltpu.CompilerParams(vmem_limit_bytes=32 * 2**20),
        cost_estimate=pl.CostEstimate(flops=flops, bytes_accessed=4 * 2**20, transcendentals=0),
    )(*scalars, *arrays)


def as_matrix(values):
    half = values.shape[-1] // 2
    return jnp.stack([values[..., :half], values[..., half:]], axis=-3)


def masked(values, rank_limit):
    keep = jnp.arange(values.shape[-2])[:, None] < jnp.asarray(rank_limit)[..., None, None]
    return jnp.where(keep, values, jnp.zeros_like(values))


def select(array, position):
    return lax.dynamic_index_in_dim(array, position, 0, keepdims=False)


def body(
    inverse_root,
    inverse_upper,
    inverse_middle,
    inverse_lower,
    leaf_inverse,
    source_root,
    source_upper,
    source_middle,
    source_lower,
    leaf_source,
    update_root,
    update_upper,
    update_middle,
    leaf_update,
    slots_root,
    slots_upper,
    slots_middle,
    leaf_slots,
    basis_upper,
    basis_middle,
    basis_lower,
    leaf_basis,
    front_ranks,
    leaf_ranks,
):
    a, e, k, d = (lax.axis_index(name) for name in ("a", "e", "k", "d"))
    rank1 = front_ranks[0:2]
    rank2 = front_ranks[2:6].reshape(2, 2)
    rank3 = front_ranks[6:14].reshape(2, 2, 2)
    separator, width = source_root.shape[2:]
    rank = leaf_basis.shape[-1]
    spots = jnp.stack([a, e, k, d]).astype(jnp.int32)

    leaf_forward, packs = call(
        leaf_kernel,
        [leaf_source.shape[2:], (8, 128, width)],
        [leaf_ranks],
        [leaf_inverse, leaf_source, leaf_basis, leaf_update, leaf_slots],
        10**9,
    )
    shared = exchange(packs, ("c",))

    keep, send, lows = call(
        apply_kernel,
        [(16, 64, width), (16, 64, width), (4, rank, width)],
        [spots],
        [
            inverse_root,
            inverse_upper,
            inverse_middle,
            source_root,
            source_upper,
            source_middle,
            update_root,
            update_upper,
            update_middle,
            slots_root,
            slots_upper,
            slots_middle,
            basis_upper,
            basis_middle,
        ],
        4 * 10**9,
    )
    applied_pieces = keep + partner(send, "k")
    keep, send, rows = call(
        lower_kernel,
        [(16, 8, width), (16, 8, width), (rank, 8, width)],
        [spots],
        [shared, inverse_lower, source_lower, basis_lower, lows],
        10**9,
    )
    lower_pieces = keep + partner(send, "k")

    rows = exchange(rows, PLANE).reshape(2, 2, 8, 8, width).sum(axis=(0, 2))
    rows = jnp.concatenate(
        [rows[:, 0], rows[:, 1], rows[:, 2], (rows[0, 3:5] + rows[1, 3:5])], axis=0
    )
    pieces = jnp.concatenate(
        [jnp.broadcast_to(rows[None], (16, 8, width)), lower_pieces, applied_pieces], axis=1
    )
    slices = exchange(pieces, CHIPS).reshape(2, 2, 4, 80, width).sum(axis=2)
    sums = slices[:, :, 16:].sum(axis=1)
    got = slices[:, :, :16]
    lower_slices = got[:, :, 8:]
    merged = got.sum(axis=1)
    rows = jnp.concatenate(
        [
            got[:, :, 0:2].reshape(8, width),
            merged[:, 2:4].reshape(4, width),
            merged[:, 4:6].reshape(4, width),
            merged[:, 6],
            merged[:, 7],
            jnp.zeros((4, width), jnp.float32),
        ],
        axis=0,
    )
    gains = share(rows, PLANE, 32)
    blocks = jnp.transpose(gains, (1, 0, 2))
    coeffs3 = masked(blocks[0:8].reshape(2, 2, 2, rank, width), rank3)
    total2 = blocks[8:12].reshape(2, 2, rank, width)
    gain2 = as_matrix(blocks[12:16].reshape(2, 2, rank, width))
    total1 = blocks[16:18]
    gain1 = as_matrix(blocks[18:20])
    pairs3 = jnp.transpose(coeffs3, (0, 2, 1, 3, 4)).reshape(2, 2, 2 * rank, width)
    coeffs2 = masked(total2 - product(gain2, pairs3), rank2)
    pairs2 = coeffs2.reshape(2, 2 * rank, width)
    coeffs1 = masked(total1 - product(gain1, pairs2), rank1)
    pair1 = coeffs1.reshape(2 * rank, width)

    first = a == 0
    wide = jnp.where(first, jnp.broadcast_to(sums.sum(axis=0), sums.shape), sums)[:, :48]
    wide_below = jnp.where(
        first, pair1[None], lax.dynamic_index_in_dim(pairs3, d, 1, keepdims=False)
    )
    wide_map = as_matrix(wide[:, 24:])
    wide_forward = wide[:, :24] - product(wide_map, wide_below)
    upper_map = as_matrix(sums[:, 56:])
    upper_forward = sums[:, 48:56] - product(upper_map, pairs2)

    wide_low = product_back(wide_map, wide_forward).reshape(4, rank, width)
    upper_low = product_back(upper_map, upper_forward).reshape(4, rank, width)
    rows = jnp.transpose(jnp.concatenate([wide_low, upper_low], axis=0), (1, 0, 2))
    rows = exchange(rows, PLANE).reshape(2, 2, 8, 8, width).sum(axis=(0, 2))
    joined = rows[0] + rows[1]
    nothing = jnp.zeros((1, width), jnp.float32)
    tail = jnp.zeros((4, width), jnp.float32)
    pieces = jnp.stack(
        [
            jnp.stack(
                [
                    jnp.concatenate(
                        [
                            wide_forward[to_a],
                            upper_forward[to_a],
                            lower_slices[to_a, to_e],
                            jnp.where(
                                first,
                                jnp.concatenate([joined[to_a : to_a + 1], nothing], axis=0),
                                rows[:, 2 * to_a + to_e],
                            ),
                            joined[4 + 2 * to_a : 6 + 2 * to_a],
                            tail,
                        ],
                        axis=0,
                    )
                    for to_e in range(2)
                ]
            )
            for to_a in range(2)
        ]
    )
    pieces = jnp.broadcast_to(pieces[:, :, None], (2, 2, 4, 48, width)).reshape(16, 48, width)
    got = exchange(pieces, CHIPS)
    half_rows = separator // 2
    mine = jnp.concatenate(
        [
            got[:8, :24].reshape(separator, width),
            got[8:, :24].reshape(separator, width),
            got[:, 24:32].reshape(128, width)[:half_rows],
            got[:, 32:40].reshape(128, width)[:half_rows],
        ],
        axis=0,
    )
    theirs = partner(mine, "k")
    lows = got[:, 40:44].reshape(2, 8, 4, width).sum(axis=1)
    upper_rows = lows[0, 2:] + lows[1, 2:]
    pieces = jnp.stack(
        [
            jnp.concatenate(
                [lows[0, :1], upper_rows[to_d : to_d + 1], lows[1, to_d : to_d + 1], nothing],
                axis=0,
            )
            for to_d in range(2)
        ]
    )
    pieces = jnp.broadcast_to(pieces[None, :, None], (2, 2, 8, 4, width)).reshape(32, 4, width)
    low_rows = exchange(pieces, PLANE)

    (pieces,) = call(
        backward_kernel,
        [(8, 128, width)],
        [spots, front_ranks],
        [
            gains,
            low_rows,
            mine,
            theirs,
            inverse_root,
            inverse_upper,
            inverse_middle,
            inverse_lower,
            basis_upper,
            basis_middle,
            basis_lower,
            shared,
        ],
        3 * 10**9,
    )
    total = exchange(pieces, ("c",)).sum(axis=0)
    tops = total[:48].reshape(2, 24, width)
    tops = select(tops, d) + partner(select(tops, 1 - d), "d")
    (leaf_solution,) = call(
        last_kernel,
        [leaf_source.shape],
        [leaf_ranks],
        [total[96:], leaf_forward, leaf_inverse, leaf_basis],
        10**9,
    )
    return (
        tops[None, None, :12],
        tops[None, None, 12:],
        total[None, None, 48:72],
        total[None, None, 72:96],
        leaf_solution,
    )


def solution(mesh):
    fine = Mesh(mesh.devices.reshape(2, 2, 4, 2, 2, 8), ROW + COL)
    tile = (ROW, COL)
    in_specs = (
        [P(*tile, None, None, None)] * 5
        + [P(ROW, None, None, None)] * 4
        + [P(*tile, None, None)]
        + [P(ROW, None, None, None, None, None)] * 3
        + [P(*tile, None, None, None)]
        + [P(ROW, None, None, None)] * 3
        + [P(*tile, None)]
        + [P(COL, None, None, None, None)] * 3
        + [P(*tile, None, None, None), P(), P(*tile)]
    )
    return jax.shard_map(
        body,
        mesh=fine,
        in_specs=tuple(in_specs),
        out_specs=(P(*tile, None, None),) * 5,
        check_vma=False,
    )
```

```python
import jax
import jax.numpy as jnp
from jax import lax
from jax.experimental import pallas as pl
from jax.experimental.pallas import tpu as pltpu
from jax.sharding import Mesh, PartitionSpec as P

precise = lax.Precision.HIGHEST

ROW = ("a", "e", "z", "k")
COL = ("d", "c")
CHIPS = ("a", "e", "z")
PLANE = ("k", "d", "c")


def exchange(pieces, axes):
    return lax.all_to_all(pieces, axes, 0, 0)


def partner(values, axis):
    return lax.ppermute(values, axis, [(0, 1), (1, 0)])


def turned(values):
    groups = []
    for at in range(0, values.shape[-1], 128):
        groups += [-values[:, at + 64 : at + 128], values[:, at : at + 64]]
    return jnp.concatenate(groups, axis=-1)


def dot(left, right, contract=1):
    return lax.dot_general(
        left,
        right,
        (((contract,), (0,)), ((), ())),
        precision=precise,
        preferred_element_type=jnp.float32,
    )


def times(real, imag, vector):
    return dot(real, vector) + dot(imag, turned(vector))


def times_back(real, imag, vector):
    return dot(real, vector, 0) + dot(imag, turned(vector), 0)


def cut(values, limit):
    rows = lax.broadcasted_iota(jnp.int32, values.shape, 0)
    return jnp.where(rows < limit, values, jnp.zeros_like(values))


def leaf_kernel(ranks, forward, packs, inverse, source, basis, update, slots):
    inner = inverse.shape[-1]
    result = times(inverse[0, 0, 0], inverse[0, 0, 1], source[0, 0])
    forward[...] = result
    low = cut(times(basis[0, 0, 0], basis[0, 0, 1], result), ranks[0, 0])
    height = inner // 2
    places = lax.broadcasted_iota(jnp.int32, (height, slots.shape[-1]), 0)
    onehot = (places == slots[0]).astype(jnp.float32)
    flat = jnp.concatenate([update[0, 0, 0], update[0, 0, 1]], axis=0)
    spread_out = lax.dot_general(
        flat,
        onehot,
        (((1,), (1,)), ((), ())),
        precision=precise,
        preferred_element_type=jnp.float32,
    )
    half = low.shape[0]
    pack = jnp.concatenate(
        [
            low,
            spread_out[:, :128],
            jnp.concatenate([spread_out[:half, 128:], spread_out[half:, 128:]], axis=-1),
        ],
        axis=0,
    )
    for place in range(packs.shape[0]):
        packs[place] = pack


def apply_kernel(
    spots,
    keep,
    send,
    lows,
    inverse0,
    inverse1,
    inverse2,
    source0,
    source1,
    source2,
    update0,
    update1,
    update2,
    slots0,
    slots1,
    slots2,
    basis1,
    basis2,
):
    a, k, d = spots[0], spots[2], spots[3]
    results = []
    for inverse, source, update, slots, at in (
        (inverse0, source0, update0, slots0, 0),
        (inverse1, source1, update1, slots1, 0),
        (inverse2, source2, update2, slots2, d),
    ):
        right = source[0, at]
        height = right.shape[0]
        lists = slots[0, at]
        places = lax.broadcasted_iota(jnp.int32, (height, lists.shape[-1]), 0)
        spread_out = jnp.zeros((height, 128), jnp.float32)
        for child in range(2):
            onehot = (places == lists[child : child + 1]).astype(jnp.float32)
            real, imag = update[0, at, child, 0], update[0, at, child, 1]
            nothing = jnp.zeros_like(real)
            order = [real, nothing, imag, nothing] if child == 0 else [nothing, real, nothing, imag]
            spread_out += lax.dot_general(
                onehot,
                jnp.concatenate(order, axis=0),
                (((1,), (1,)), ((), ())),
                precision=precise,
                preferred_element_type=jnp.float32,
            )
        both = jnp.concatenate([right, spread_out], axis=-1)
        apply = times if inverse is inverse1 else times_back
        results.append(apply(inverse[0, 0, 0], inverse[0, 0, 1], both))
    low2 = times(basis2[0, a, 0], basis2[0, a, 1], results[2])
    low1 = times(basis1[0, a, 0], basis1[0, a, 1], results[1])
    lows[0] = low2[:, :128]
    lows[1] = low2[:, 128:]
    lows[2] = low1[:, :128]
    lows[3] = low1[:, 128:]

    def put(target, half):
        for side in range(2):
            for level, at in ((0, 0), (2, 8)):
                rows = results[level].shape[0] // 2
                part = results[level][half * rows : (half + 1) * rows, side * 128 : side * 128 + 128]
                target[at : at + 8, 24 * side : 24 * side + 24] = part.reshape(8, 24, 128)
            rows = results[1].shape[0] // 2
            part = results[1][half * rows : (half + 1) * rows, side * 128 : side * 128 + 128]
            row = 48 + 8 * side
            target[0:12, row : row + 8] = part.reshape(12, 8, 128)
            target[12:16, row : row + 8] = jnp.zeros((4, 8, 128), jnp.float32)

    for half in range(2):

        @pl.when(k == half)
        def _(half=half):
            put(keep, half)
            put(send, 1 - half)


def lower_kernel(spots, shared, lows, keep, send, rows, inverse, source, basis):
    a, e, k, d = spots[0], spots[1], spots[2], spots[3]
    low = shared[:, 0:32].reshape(256, 128)
    low_turned = turned(low)
    packs = shared[:, 96:128].reshape(256, 128)
    top = dot(shared[:, 32:64].reshape(256, 128), low, 0) + dot(
        shared[:, 64:96].reshape(256, 128), low_turned, 0
    )
    rest = dot(packs[:, :64], low, 0) + dot(packs[:, 64:], low_turned, 0)
    side = source[0, d] - jnp.concatenate([top, rest], axis=0)
    partial = times(inverse[0, 0, 0], inverse[0, 0, 1], side)
    front = 2 * a + e
    low3 = times(basis[0, front, 0], basis[0, front, 1], partial)
    rows[:, 0, :] = low3
    for at in range(4):
        rows[:, at + 1, :] = lows[at]
    for at in range(5, 8):
        rows[:, at, :] = jnp.zeros((32, 128), jnp.float32)
    count = partial.shape[0] // 2

    def put(target, half):
        target[0:12] = partial[half * count : (half + 1) * count].reshape(12, 8, 128)
        target[12:16] = jnp.zeros((4, 8, 128), jnp.float32)

    for half in range(2):

        @pl.when(k == half)
        def _(half=half):
            put(keep, half)
            put(send, 1 - half)


def backward_kernel(
    spots,
    ranks,
    gains,
    lows,
    mine,
    theirs,
    inverse0,
    inverse1,
    inverse2,
    inverse3,
    basis1,
    basis2,
    basis3,
    shared,
    pieces,
):
    a, e, k, d = spots[0], spots[1], spots[2], spots[3]

    def gain_back(gain, low, child):
        both = times_back(gain[:, :64], gain[:, 64:], low)
        return jnp.where(child == 0, both[:32], both[32:])

    gain1 = jnp.where(a == 0, gains[:, 18, :], gains[:, 19, :])
    gain2 = jnp.where(
        a == 0,
        jnp.where(d == 0, gains[:, 12, :], gains[:, 13, :]),
        jnp.where(d == 0, gains[:, 14, :], gains[:, 15, :]),
    )
    back1 = cut(lows[:, 0, :], ranks[a])
    back2 = cut(lows[:, 1, :] - gain_back(gain1, back1, d), ranks[2 + 2 * a + d])
    back3 = cut(lows[:, 2, :] - gain_back(gain2, back2, e), ranks[6 + 4 * a + 2 * e + d])

    def whole(start, stop):
        left, right = mine[start:stop], theirs[start:stop]
        return jnp.concatenate(
            [jnp.where(k == 0, left, right), jnp.where(k == 0, right, left)], axis=0
        )

    front = 2 * a + e
    residuals = (
        whole(0, 192),
        whole(384, 480) - times_back(basis1[0, a, 0], basis1[0, a, 1], back1),
        whole(192, 384) - times_back(basis2[0, a, 0], basis2[0, a, 1], back2),
        whole(480, 576) - times_back(basis3[0, front, 0], basis3[0, front, 1], back3),
    )
    solved = [
        times(inverse0[0, 0, 0], inverse0[0, 0, 1], residuals[0]),
        times_back(inverse1[0, 0, 0], inverse1[0, 0, 1], residuals[1]),
        times(inverse2[0, 0, 0], inverse2[0, 0, 1], residuals[2]),
        times_back(inverse3[0, 0, 0], inverse3[0, 0, 1], residuals[3]),
    ]
    for level in range(2):
        for place in range(2):
            for to_c in range(8):
                at = 96 * place + 12 * to_c
                row = 24 * place + 12 * level
                pieces[to_c, row : row + 12] = solved[level][at : at + 12]
    pieces[:, 48:72] = solved[2].reshape(8, 24, 128)
    pieces[:, 72:96] = solved[3].reshape(8, 24, 128)
    lowest = solved[3]
    lowest_turned = turned(lowest)
    packs = shared[:, 96:128].reshape(256, 128)
    parts = (
        dot(shared[:, 32:64].reshape(256, 128), lowest[:128])
        + dot(shared[:, 64:96].reshape(256, 128), lowest_turned[:128])
        + dot(packs[:, :64], lowest[128:])
        + dot(packs[:, 64:], lowest_turned[128:])
    )
    pieces[:, 96:128] = parts.reshape(8, 32, 128)


def last_kernel(ranks, low, forward, inverse, basis, solved):
    back = cut(low[...], ranks[0, 0])
    rest = forward[...] - times_back(basis[0, 0, 0], basis[0, 0, 1], back)
    solved[0, 0] = times_back(inverse[0, 0, 0], inverse[0, 0, 1], rest)


def gather_kernel(parts, applied_keep, applied_got, lower_keep, lower_got, pieces):
    sums = []
    for place in range(2):
        total = jnp.zeros((8, 128), jnp.float32)
        for core in range(2):
            for at in range(8):
                total += parts[16 * core + 8 * place + at]
        sums.append(total)
    rows = [sums[place][row : row + 1] for row in range(3) for place in range(2)]
    rows += [sums[0][3:5] + sums[1][3:5]]
    tile = jnp.concatenate(rows, axis=0)
    for chip in range(16):
        pieces[chip, 0:8] = tile
        pieces[chip, 8:16] = lower_keep[chip] + lower_got[chip]
        pieces[chip, 16:80] = applied_keep[chip] + applied_got[chip]


def total_kernel(parts, pieces, sums, lower):
    tiles = []
    for at in range(4):
        total = parts[4 * at]
        for chip in range(1, 4):
            total += parts[4 * at + chip]
        tiles.append(total)
        lower[at] = total[8:16]
    upper = []
    for place in range(2):
        total = tiles[2 * place] + tiles[2 * place + 1]
        sums[place] = total[16:80]
        upper.append(total)
    rows = [tile[0:2] for tile in tiles]
    for start, stop in ((2, 4), (4, 6), (6, 7), (7, 8)):
        rows += [total[start:stop] for total in upper]
    rows += [jnp.zeros((4, 128), jnp.float32)]
    tile = jnp.concatenate(rows, axis=0)
    for place in range(32):
        pieces[place] = tile


def forward_kernel(spots, ranks, gains, sums, wide_out, upper_out, rows):
    a, d = spots[0], spots[3]
    coeffs3 = [cut(gains[:, at, :], ranks[6 + at]) for at in range(8)]
    pairs3 = [
        [jnp.concatenate([coeffs3[4 * x + y], coeffs3[4 * x + 2 + y]], axis=0) for y in range(2)]
        for x in range(2)
    ]

    def chain(total, gain, pair, limit):
        return cut(total - times(gain[:, :64], gain[:, 64:], pair), limit)

    pairs2 = []
    for x in range(2):
        both = [
            chain(
                gains[:, 8 + 2 * x + y, :],
                gains[:, 12 + 2 * x + y, :],
                pairs3[x][y],
                ranks[2 + 2 * x + y],
            )
            for y in range(2)
        ]
        pairs2.append(jnp.concatenate(both, axis=0))
    pair1 = jnp.concatenate(
        [chain(gains[:, 16 + x, :], gains[:, 18 + x, :], pairs2[x], ranks[x]) for x in range(2)],
        axis=0,
    )
    everything = sums[0, 0:48] + sums[1, 0:48]
    for x in range(2):
        below = jnp.where(a == 0, pair1, jnp.where(d == 0, pairs3[x][0], pairs3[x][1]))
        slices = jnp.where(a == 0, everything, sums[x, 0:48])
        gain = slices[24:48]
        result = slices[0:24] - times(gain[:, :64], gain[:, 64:], below)
        wide_out[x] = result
        low = times_back(gain[:, :64], gain[:, 64:], result)
        rows[:, 2 * x, :] = low[:32]
        rows[:, 2 * x + 1, :] = low[32:]
        gain = sums[x, 56:64]
        result = sums[x, 48:56] - times(gain[:, :64], gain[:, 64:], pairs2[x])
        upper_out[x] = result
        low = times_back(gain[:, :64], gain[:, 64:], result)
        rows[:, 4 + 2 * x, :] = low[:32]
        rows[:, 5 + 2 * x, :] = low[32:]


def slices_kernel(spots, parts, wide, upper, lower, pieces):
    a = spots[0]
    sums = []
    for place in range(2):
        total = jnp.zeros((8, 128), jnp.float32)
        for core in range(2):
            for at in range(8):
                total += parts[16 * core + 8 * place + at]
        sums.append(total)
    joined = sums[0] + sums[1]
    nothing = jnp.zeros((1, 128), jnp.float32)
    for to_a in range(2):
        for to_e in range(2):
            row = 2 * to_a + to_e
            tile = jnp.concatenate(
                [
                    jnp.where(a == 0, joined[to_a : to_a + 1], sums[0][row : row + 1]),
                    jnp.where(a == 0, nothing, sums[1][row : row + 1]),
                    joined[4 + 2 * to_a : 6 + 2 * to_a],
                    jnp.zeros((4, 128), jnp.float32),
                ],
                axis=0,
            )
            for chip in range(4):
                place = 8 * to_a + 4 * to_e + chip
                pieces[place, 0:24] = wide[to_a]
                pieces[place, 24:32] = upper[to_a]
                pieces[place, 32:40] = lower[row]
                pieces[place, 40:48] = tile


def arrange_kernel(parts, mine, pieces):
    for chip in range(8):
        mine[24 * chip : 24 * chip + 24] = parts[chip, 0:24]
        mine[192 + 24 * chip : 216 + 24 * chip] = parts[8 + chip, 0:24]
    for chip in range(12):
        mine[384 + 8 * chip : 392 + 8 * chip] = parts[chip, 24:32]
        mine[480 + 8 * chip : 488 + 8 * chip] = parts[chip, 32:40]
    sums = []
    for place in range(2):
        total = parts[8 * place, 40:48]
        for chip in range(1, 8):
            total += parts[8 * place + chip, 40:48]
        sums.append(total)
    upper = sums[0] + sums[1]
    tail = jnp.zeros((5, 128), jnp.float32)
    for to_d in range(2):
        tile = jnp.concatenate(
            [sums[0][0:1], upper[2 + to_d : 3 + to_d], sums[1][to_d : to_d + 1], tail], axis=0
        )
        for core in range(2):
            for to_c in range(8):
                pieces[16 * core + 8 * to_d + to_c] = tile


def flipped(values):
    return jnp.swapaxes(values, -1, -2)


def call(kernel, shapes, scalars, arrays, flops, fetched=()):
    count = len(fetched)
    before = len(scalars) + len(arrays)

    def outer(*refs):
        inputs, sources = refs[:before], refs[before : before + count]
        outputs = refs[before + count : before + count + len(shapes)]
        buffers = refs[before + count + len(shapes) :]
        if count:
            sems = buffers[-1]
            copies = [
                pltpu.make_async_copy(source, buffer, sems.at[at])
                for at, (source, buffer) in enumerate(zip(sources, buffers[:-1]))
            ]
            for copy in copies:
                copy.start()
            for copy in copies:
                copy.wait()
        kernel(*inputs, *outputs, *buffers[:count])

    scratch = [pltpu.VMEM(array.shape, array.dtype) for array in fetched]
    if count:
        scratch.append(pltpu.SemaphoreType.DMA((count,)))
    return pl.pallas_call(
        outer,
        out_shape=[jax.ShapeDtypeStruct(shape, jnp.float32) for shape in shapes],
        in_specs=[pl.BlockSpec(memory_space=pltpu.SMEM)] * len(scalars)
        + [pl.BlockSpec(memory_space=pltpu.VMEM)] * len(arrays)
        + [pl.BlockSpec(memory_space=pltpu.HBM)] * count,
        out_specs=[pl.BlockSpec(memory_space=pltpu.VMEM)] * len(shapes),
        scratch_shapes=scratch,
        compiler_params=pltpu.CompilerParams(vmem_limit_bytes=24 * 2**20),
        cost_estimate=pl.CostEstimate(flops=flops, bytes_accessed=4 * 2**20, transcendentals=0),
    )(*scalars, *arrays, *fetched)


def select(array, position):
    return lax.dynamic_index_in_dim(array, position, 0, keepdims=False)


def body(
    inverse_root,
    inverse_upper,
    inverse_middle,
    inverse_lower,
    leaf_inverse,
    source_root,
    source_upper,
    source_middle,
    source_lower,
    leaf_source,
    update_root,
    update_upper,
    update_middle,
    leaf_update,
    slots_root,
    slots_upper,
    slots_middle,
    leaf_slots,
    basis_upper,
    basis_middle,
    basis_lower,
    leaf_basis,
    front_ranks,
    leaf_ranks,
):
    a, e, k, d = (lax.axis_index(name) for name in ("a", "e", "k", "d"))
    separator, width = source_root.shape[2:]
    rank = leaf_basis.shape[-1]
    spots = jnp.stack([a, e, k, d]).astype(jnp.int32)

    leaf_forward, packs = call(
        leaf_kernel,
        [leaf_source.shape[2:], (8, 128, width)],
        [leaf_ranks],
        [],
        10**9,
        [leaf_inverse, leaf_source, flipped(leaf_basis), flipped(leaf_update), leaf_slots],
    )
    shared = exchange(packs, ("c",))

    keep, send, lows = call(
        apply_kernel,
        [(16, 64, width), (16, 64, width), (4, rank, width)],
        [spots],
        [],
        4 * 10**9,
        [
            flipped(inverse_root),
            inverse_upper,
            flipped(inverse_middle),
            source_root,
            source_upper,
            source_middle,
            flipped(update_root),
            flipped(update_upper),
            flipped(update_middle),
            slots_root,
            slots_upper,
            slots_middle,
            flipped(basis_upper),
            flipped(basis_middle),
        ],
    )
    applied = (keep, partner(send, "k"))
    keep, send, rows = call(
        lower_kernel,
        [(16, 8, width), (16, 8, width), (rank, 8, width)],
        [spots],
        [shared, lows],
        10**9,
        [inverse_lower, source_lower, flipped(basis_lower)],
    )
    lower = (keep, partner(send, "k"))

    parts = exchange(rows, PLANE)
    (pieces,) = call(gather_kernel, [(16, 80, width)], [], [parts, *applied, *lower], 10**7)
    parts = exchange(pieces, CHIPS)
    pieces, sums, lower_slices = call(
        total_kernel, [(32, 24, width), (2, 64, width), (4, 8, width)], [], [parts], 10**7
    )
    gains = exchange(pieces, PLANE)

    wide, upper, rows = call(
        forward_kernel,
        [(2, 24, width), (2, 8, width), (rank, 8, width)],
        [spots, front_ranks],
        [gains, sums],
        10**8,
    )
    parts = exchange(rows, PLANE)
    (pieces,) = call(
        slices_kernel, [(16, 48, width)], [spots], [parts, wide, upper, lower_slices], 10**7
    )
    parts = exchange(pieces, CHIPS)
    mine, pieces = call(
        arrange_kernel, [(3 * separator, width), (32, 8, width)], [], [parts], 10**7
    )
    theirs = partner(mine, "k")
    low_rows = exchange(pieces, PLANE)

    (pieces,) = call(
        backward_kernel,
        [(8, 128, width)],
        [spots, front_ranks],
        [
            gains,
            low_rows,
            mine,
            theirs,
            flipped(inverse_root),
            inverse_upper,
            flipped(inverse_middle),
            inverse_lower,
            flipped(basis_upper),
            flipped(basis_middle),
            flipped(basis_lower),
            shared,
        ],
        3 * 10**9,
    )
    total = exchange(pieces, ("c",)).sum(axis=0)
    tops = total[:48].reshape(2, 24, width)
    tops = select(tops, d) + partner(select(tops, 1 - d), "d")
    (leaf_solution,) = call(
        last_kernel,
        [leaf_source.shape],
        [leaf_ranks],
        [total[96:], leaf_forward, leaf_inverse, flipped(leaf_basis)],
        10**9,
    )
    return (
        tops[None, None, :12],
        tops[None, None, 12:],
        total[None, None, 48:72],
        total[None, None, 72:96],
        leaf_solution,
    )


def solution(mesh):
    fine = Mesh(mesh.devices.reshape(2, 2, 4, 2, 2, 8), ROW + COL)
    tile = (ROW, COL)
    in_specs = (
        [P(*tile, None, None, None)] * 5
        + [P(ROW, None, None, None)] * 4
        + [P(*tile, None, None)]
        + [P(ROW, None, None, None, None, None)] * 3
        + [P(*tile, None, None, None)]
        + [P(ROW, None, None, None)] * 3
        + [P(*tile, None)]
        + [P(COL, None, None, None, None)] * 3
        + [P(*tile, None, None, None), P(), P(*tile)]
    )
    return jax.shard_map(
        body,
        mesh=fine,
        in_specs=tuple(in_specs),
        out_specs=(P(*tile, None, None),) * 5,
        check_vma=False,
    )
```

```python
import jax
import jax.numpy as jnp
from jax import lax
from jax.experimental import pallas as pl
from jax.experimental.pallas import tpu as pltpu
from jax.sharding import Mesh, PartitionSpec as P

precise = lax.Precision.HIGHEST

ROW = ("a", "e", "z", "k")
COL = ("d", "c")
CHIPS = ("a", "e", "z")
PLANE = ("k", "d", "c")


def exchange(pieces, axes):
    return lax.all_to_all(pieces, axes, 0, 0)


def partner(values, axis):
    return lax.ppermute(values, axis, [(0, 1), (1, 0)])


def turned(values):
    groups = []
    for at in range(0, values.shape[-1], 128):
        groups += [-values[:, at + 64 : at + 128], values[:, at : at + 64]]
    return jnp.concatenate(groups, axis=-1)


def halves(values):
    high = values.astype(jnp.bfloat16)
    return high, (values - high.astype(jnp.float32)).astype(jnp.bfloat16)


def dot(left, right, contract=1):
    left_high, left_low = halves(left)
    right_high, right_low = halves(right)

    def one(x, y):
        return lax.dot_general(
            x, y, (((contract,), (0,)), ((), ())), preferred_element_type=jnp.float32
        )

    return one(left_high, right_high) + (one(left_high, right_low) + one(left_low, right_high))


def times(real, imag, vector):
    return dot(real, vector) + dot(imag, turned(vector))


def times_back(real, imag, vector):
    return dot(real, vector, 0) + dot(imag, turned(vector), 0)


def cut(values, limit):
    rows = lax.broadcasted_iota(jnp.int32, values.shape, 0)
    return jnp.where(rows < limit, values, jnp.zeros_like(values))


def leaf_kernel(ranks, forward, packs, inverse, source, basis, update, slots):
    inner = inverse.shape[-1]
    result = times(inverse[0, 0, 0], inverse[0, 0, 1], source[0, 0])
    forward[...] = result
    low = cut(times(basis[0, 0, 0], basis[0, 0, 1], result), ranks[0, 0])
    height = inner // 2
    places = lax.broadcasted_iota(jnp.int32, (height, slots.shape[-1]), 0)
    onehot = (places == slots[0]).astype(jnp.float32)
    flat = jnp.concatenate([update[0, 0, 0], update[0, 0, 1]], axis=0)
    spread_out = lax.dot_general(
        flat,
        onehot,
        (((1,), (1,)), ((), ())),
        precision=precise,
        preferred_element_type=jnp.float32,
    )
    half = low.shape[0]
    pack = jnp.concatenate(
        [
            low,
            spread_out[:, :128],
            jnp.concatenate([spread_out[:half, 128:], spread_out[half:, 128:]], axis=-1),
        ],
        axis=0,
    )
    for place in range(packs.shape[0]):
        packs[place] = pack


def apply_kernel(
    spots,
    keep,
    send,
    lows,
    inverse0,
    inverse1,
    inverse2,
    source0,
    source1,
    source2,
    update0,
    update1,
    update2,
    slots0,
    slots1,
    slots2,
    basis1,
    basis2,
):
    a, k, d = spots[0], spots[2], spots[3]
    results = []
    for inverse, source, update, slots, at in (
        (inverse0, source0, update0, slots0, 0),
        (inverse1, source1, update1, slots1, 0),
        (inverse2, source2, update2, slots2, d),
    ):
        right = source[0, at]
        height = right.shape[0]
        lists = slots[0, at]
        places = lax.broadcasted_iota(jnp.int32, (height, lists.shape[-1]), 0)
        spread_out = jnp.zeros((height, 128), jnp.float32)
        for child in range(2):
            onehot = (places == lists[child : child + 1]).astype(jnp.float32)
            real, imag = update[0, at, child, 0], update[0, at, child, 1]
            nothing = jnp.zeros_like(real)
            order = [real, nothing, imag, nothing] if child == 0 else [nothing, real, nothing, imag]
            spread_out += lax.dot_general(
                onehot,
                jnp.concatenate(order, axis=0),
                (((1,), (1,)), ((), ())),
                precision=precise,
                preferred_element_type=jnp.float32,
            )
        both = jnp.concatenate([right, spread_out], axis=-1)
        apply = times if inverse is inverse1 else times_back
        results.append(apply(inverse[0, 0, 0], inverse[0, 0, 1], both))
    low2 = times(basis2[0, a, 0], basis2[0, a, 1], results[2])
    low1 = times(basis1[0, a, 0], basis1[0, a, 1], results[1])
    lows[0] = low2[:, :128]
    lows[1] = low2[:, 128:]
    lows[2] = low1[:, :128]
    lows[3] = low1[:, 128:]

    def put(target, half):
        for side in range(2):
            for level, at in ((0, 0), (2, 8)):
                rows = results[level].shape[0] // 2
                part = results[level][half * rows : (half + 1) * rows, side * 128 : side * 128 + 128]
                target[at : at + 8, 24 * side : 24 * side + 24] = part.reshape(8, 24, 128)
            rows = results[1].shape[0] // 2
            part = results[1][half * rows : (half + 1) * rows, side * 128 : side * 128 + 128]
            row = 48 + 8 * side
            target[0:12, row : row + 8] = part.reshape(12, 8, 128)
            target[12:16, row : row + 8] = jnp.zeros((4, 8, 128), jnp.float32)

    for half in range(2):

        @pl.when(k == half)
        def _(half=half):
            put(keep, half)
            put(send, 1 - half)


def lower_kernel(spots, shared, lows, keep, send, rows, inverse, source, basis):
    a, e, k, d = spots[0], spots[1], spots[2], spots[3]
    low = shared[:, 0:32].reshape(256, 128)
    low_turned = turned(low)
    packs = shared[:, 96:128].reshape(256, 128)
    top = dot(shared[:, 32:64].reshape(256, 128), low, 0) + dot(
        shared[:, 64:96].reshape(256, 128), low_turned, 0
    )
    rest = dot(packs[:, :64], low, 0) + dot(packs[:, 64:], low_turned, 0)
    side = source[0, d] - jnp.concatenate([top, rest], axis=0)
    partial = times(inverse[0, 0, 0], inverse[0, 0, 1], side)
    front = 2 * a + e
    low3 = times(basis[0, front, 0], basis[0, front, 1], partial)
    rows[:, 0, :] = low3
    for at in range(4):
        rows[:, at + 1, :] = lows[at]
    for at in range(5, 8):
        rows[:, at, :] = jnp.zeros((32, 128), jnp.float32)
    count = partial.shape[0] // 2

    def put(target, half):
        target[0:12] = partial[half * count : (half + 1) * count].reshape(12, 8, 128)
        target[12:16] = jnp.zeros((4, 8, 128), jnp.float32)

    for half in range(2):

        @pl.when(k == half)
        def _(half=half):
            put(keep, half)
            put(send, 1 - half)


def backward_kernel(
    spots,
    ranks,
    gains,
    lows,
    mine,
    theirs,
    inverse0,
    inverse1,
    inverse2,
    inverse3,
    basis1,
    basis2,
    basis3,
    shared,
    pieces,
):
    a, e, k, d = spots[0], spots[1], spots[2], spots[3]

    def gain_back(gain, low, child):
        both = times_back(gain[:, :64], gain[:, 64:], low)
        return jnp.where(child == 0, both[:32], both[32:])

    gain1 = jnp.where(a == 0, gains[:, 18, :], gains[:, 19, :])
    gain2 = jnp.where(
        a == 0,
        jnp.where(d == 0, gains[:, 12, :], gains[:, 13, :]),
        jnp.where(d == 0, gains[:, 14, :], gains[:, 15, :]),
    )
    back1 = cut(lows[:, 0, :], ranks[a])
    back2 = cut(lows[:, 1, :] - gain_back(gain1, back1, d), ranks[2 + 2 * a + d])
    back3 = cut(lows[:, 2, :] - gain_back(gain2, back2, e), ranks[6 + 4 * a + 2 * e + d])

    def whole(start, stop):
        left, right = mine[start:stop], theirs[start:stop]
        return jnp.concatenate(
            [jnp.where(k == 0, left, right), jnp.where(k == 0, right, left)], axis=0
        )

    front = 2 * a + e
    residuals = (
        whole(0, 192),
        whole(384, 480) - times_back(basis1[0, a, 0], basis1[0, a, 1], back1),
        whole(192, 384) - times_back(basis2[0, a, 0], basis2[0, a, 1], back2),
        whole(480, 576) - times_back(basis3[0, front, 0], basis3[0, front, 1], back3),
    )
    solved = [
        times(inverse0[0, 0, 0], inverse0[0, 0, 1], residuals[0]),
        times_back(inverse1[0, 0, 0], inverse1[0, 0, 1], residuals[1]),
        times(inverse2[0, 0, 0], inverse2[0, 0, 1], residuals[2]),
        times_back(inverse3[0, 0, 0], inverse3[0, 0, 1], residuals[3]),
    ]
    for level in range(2):
        for place in range(2):
            for to_c in range(8):
                at = 96 * place + 12 * to_c
                row = 24 * place + 12 * level
                pieces[to_c, row : row + 12] = solved[level][at : at + 12]
    pieces[:, 48:72] = solved[2].reshape(8, 24, 128)
    pieces[:, 72:96] = solved[3].reshape(8, 24, 128)
    lowest = solved[3]
    lowest_turned = turned(lowest)
    packs = shared[:, 96:128].reshape(256, 128)
    parts = (
        dot(shared[:, 32:64].reshape(256, 128), lowest[:128])
        + dot(shared[:, 64:96].reshape(256, 128), lowest_turned[:128])
        + dot(packs[:, :64], lowest[128:])
        + dot(packs[:, 64:], lowest_turned[128:])
    )
    pieces[:, 96:128] = parts.reshape(8, 32, 128)


def last_kernel(ranks, low, forward, inverse, basis, solved):
    back = cut(low[...], ranks[0, 0])
    rest = forward[...] - times_back(basis[0, 0, 0], basis[0, 0, 1], back)
    solved[0, 0] = times_back(inverse[0, 0, 0], inverse[0, 0, 1], rest)


def gather_kernel(parts, applied_keep, applied_got, lower_keep, lower_got, pieces):
    sums = []
    for place in range(2):
        total = jnp.zeros((8, 128), jnp.float32)
        for core in range(2):
            for at in range(8):
                total += parts[16 * core + 8 * place + at]
        sums.append(total)
    rows = [sums[place][row : row + 1] for row in range(3) for place in range(2)]
    rows += [sums[0][3:5] + sums[1][3:5]]
    tile = jnp.concatenate(rows, axis=0)
    for chip in range(16):
        pieces[chip, 0:8] = tile
        pieces[chip, 8:16] = lower_keep[chip] + lower_got[chip]
        pieces[chip, 16:80] = applied_keep[chip] + applied_got[chip]


def total_kernel(parts, pieces, sums, lower):
    tiles = []
    for at in range(4):
        total = parts[4 * at]
        for chip in range(1, 4):
            total += parts[4 * at + chip]
        tiles.append(total)
        lower[at] = total[8:16]
    upper = []
    for place in range(2):
        total = tiles[2 * place] + tiles[2 * place + 1]
        sums[place] = total[16:80]
        upper.append(total)
    rows = [tile[0:2] for tile in tiles]
    for start, stop in ((2, 4), (4, 6), (6, 7), (7, 8)):
        rows += [total[start:stop] for total in upper]
    rows += [jnp.zeros((4, 128), jnp.float32)]
    tile = jnp.concatenate(rows, axis=0)
    for place in range(32):
        pieces[place] = tile


def forward_kernel(spots, ranks, gains, sums, wide_out, upper_out, rows):
    a, d = spots[0], spots[3]
    coeffs3 = [cut(gains[:, at, :], ranks[6 + at]) for at in range(8)]
    pairs3 = [
        [jnp.concatenate([coeffs3[4 * x + y], coeffs3[4 * x + 2 + y]], axis=0) for y in range(2)]
        for x in range(2)
    ]

    def chain(total, gain, pair, limit):
        return cut(total - times(gain[:, :64], gain[:, 64:], pair), limit)

    pairs2 = []
    for x in range(2):
        both = [
            chain(
                gains[:, 8 + 2 * x + y, :],
                gains[:, 12 + 2 * x + y, :],
                pairs3[x][y],
                ranks[2 + 2 * x + y],
            )
            for y in range(2)
        ]
        pairs2.append(jnp.concatenate(both, axis=0))
    pair1 = jnp.concatenate(
        [chain(gains[:, 16 + x, :], gains[:, 18 + x, :], pairs2[x], ranks[x]) for x in range(2)],
        axis=0,
    )
    everything = sums[0, 0:48] + sums[1, 0:48]
    for x in range(2):
        below = jnp.where(a == 0, pair1, jnp.where(d == 0, pairs3[x][0], pairs3[x][1]))
        slices = jnp.where(a == 0, everything, sums[x, 0:48])
        gain = slices[24:48]
        result = slices[0:24] - times(gain[:, :64], gain[:, 64:], below)
        wide_out[x] = result
        low = times_back(gain[:, :64], gain[:, 64:], result)
        rows[:, 2 * x, :] = low[:32]
        rows[:, 2 * x + 1, :] = low[32:]
        gain = sums[x, 56:64]
        result = sums[x, 48:56] - times(gain[:, :64], gain[:, 64:], pairs2[x])
        upper_out[x] = result
        low = times_back(gain[:, :64], gain[:, 64:], result)
        rows[:, 4 + 2 * x, :] = low[:32]
        rows[:, 5 + 2 * x, :] = low[32:]


def slices_kernel(spots, parts, wide, upper, lower, pieces):
    a = spots[0]
    sums = []
    for place in range(2):
        total = jnp.zeros((8, 128), jnp.float32)
        for core in range(2):
            for at in range(8):
                total += parts[16 * core + 8 * place + at]
        sums.append(total)
    joined = sums[0] + sums[1]
    nothing = jnp.zeros((1, 128), jnp.float32)
    for to_a in range(2):
        for to_e in range(2):
            row = 2 * to_a + to_e
            tile = jnp.concatenate(
                [
                    jnp.where(a == 0, joined[to_a : to_a + 1], sums[0][row : row + 1]),
                    jnp.where(a == 0, nothing, sums[1][row : row + 1]),
                    joined[4 + 2 * to_a : 6 + 2 * to_a],
                    jnp.zeros((4, 128), jnp.float32),
                ],
                axis=0,
            )
            for chip in range(4):
                place = 8 * to_a + 4 * to_e + chip
                pieces[place, 0:24] = wide[to_a]
                pieces[place, 24:32] = upper[to_a]
                pieces[place, 32:40] = lower[row]
                pieces[place, 40:48] = tile


def arrange_kernel(parts, mine, pieces):
    for chip in range(8):
        mine[24 * chip : 24 * chip + 24] = parts[chip, 0:24]
        mine[192 + 24 * chip : 216 + 24 * chip] = parts[8 + chip, 0:24]
    for chip in range(12):
        mine[384 + 8 * chip : 392 + 8 * chip] = parts[chip, 24:32]
        mine[480 + 8 * chip : 488 + 8 * chip] = parts[chip, 32:40]
    sums = []
    for place in range(2):
        total = parts[8 * place, 40:48]
        for chip in range(1, 8):
            total += parts[8 * place + chip, 40:48]
        sums.append(total)
    upper = sums[0] + sums[1]
    tail = jnp.zeros((5, 128), jnp.float32)
    for to_d in range(2):
        tile = jnp.concatenate(
            [sums[0][0:1], upper[2 + to_d : 3 + to_d], sums[1][to_d : to_d + 1], tail], axis=0
        )
        for core in range(2):
            for to_c in range(8):
                pieces[16 * core + 8 * to_d + to_c] = tile


def flipped(values):
    return jnp.swapaxes(values, -1, -2)


def call(kernel, shapes, scalars, arrays, flops, fetched=()):
    count = len(fetched)
    before = len(scalars) + len(arrays)

    def outer(*refs):
        inputs, sources = refs[:before], refs[before : before + count]
        outputs = refs[before + count : before + count + len(shapes)]
        buffers = refs[before + count + len(shapes) :]
        if count:
            sems = buffers[-1]
            copies = [
                pltpu.make_async_copy(source, buffer, sems.at[at])
                for at, (source, buffer) in enumerate(zip(sources, buffers[:-1]))
            ]
            for copy in copies:
                copy.start()
            for copy in copies:
                copy.wait()
        kernel(*inputs, *outputs, *buffers[:count])

    scratch = [pltpu.VMEM(array.shape, array.dtype) for array in fetched]
    if count:
        scratch.append(pltpu.SemaphoreType.DMA((count,)))
    return pl.pallas_call(
        outer,
        out_shape=[jax.ShapeDtypeStruct(shape, jnp.float32) for shape in shapes],
        in_specs=[pl.BlockSpec(memory_space=pltpu.SMEM)] * len(scalars)
        + [pl.BlockSpec(memory_space=pltpu.VMEM)] * len(arrays)
        + [pl.BlockSpec(memory_space=pltpu.HBM)] * count,
        out_specs=[pl.BlockSpec(memory_space=pltpu.VMEM)] * len(shapes),
        scratch_shapes=scratch,
        compiler_params=pltpu.CompilerParams(vmem_limit_bytes=(60 if count else 24) * 2**20),
        cost_estimate=pl.CostEstimate(flops=flops, bytes_accessed=4 * 2**20, transcendentals=0),
    )(*scalars, *arrays, *fetched)


def select(array, position):
    return lax.dynamic_index_in_dim(array, position, 0, keepdims=False)


def body(
    inverse_root,
    inverse_upper,
    inverse_middle,
    inverse_lower,
    leaf_inverse,
    source_root,
    source_upper,
    source_middle,
    source_lower,
    leaf_source,
    update_root,
    update_upper,
    update_middle,
    leaf_update,
    slots_root,
    slots_upper,
    slots_middle,
    leaf_slots,
    basis_upper,
    basis_middle,
    basis_lower,
    leaf_basis,
    front_ranks,
    leaf_ranks,
):
    a, e, k, d = (lax.axis_index(name) for name in ("a", "e", "k", "d"))
    separator, width = source_root.shape[2:]
    rank = leaf_basis.shape[-1]
    spots = jnp.stack([a, e, k, d]).astype(jnp.int32)

    leaf_forward, packs = call(
        leaf_kernel,
        [leaf_source.shape[2:], (8, 128, width)],
        [leaf_ranks],
        [],
        10**9,
        [leaf_inverse, leaf_source, flipped(leaf_basis), flipped(leaf_update), leaf_slots],
    )
    shared = exchange(packs, ("c",))

    keep, send, lows = call(
        apply_kernel,
        [(16, 64, width), (16, 64, width), (4, rank, width)],
        [spots],
        [],
        4 * 10**9,
        [
            flipped(inverse_root),
            inverse_upper,
            flipped(inverse_middle),
            source_root,
            source_upper,
            source_middle,
            flipped(update_root),
            flipped(update_upper),
            flipped(update_middle),
            slots_root,
            slots_upper,
            slots_middle,
            flipped(basis_upper),
            flipped(basis_middle),
        ],
    )
    applied = (keep, partner(send, "k"))
    keep, send, rows = call(
        lower_kernel,
        [(16, 8, width), (16, 8, width), (rank, 8, width)],
        [spots],
        [shared, lows],
        10**9,
        [inverse_lower, source_lower, flipped(basis_lower)],
    )
    lower = (keep, partner(send, "k"))

    parts = exchange(rows, PLANE)
    (pieces,) = call(gather_kernel, [(16, 80, width)], [], [parts, *applied, *lower], 10**7)
    parts = exchange(pieces, CHIPS)
    pieces, sums, lower_slices = call(
        total_kernel, [(32, 24, width), (2, 64, width), (4, 8, width)], [], [parts], 10**7
    )
    gains = exchange(pieces, PLANE)

    wide, upper, rows = call(
        forward_kernel,
        [(2, 24, width), (2, 8, width), (rank, 8, width)],
        [spots, front_ranks],
        [gains, sums],
        10**8,
    )
    parts = exchange(rows, PLANE)
    (pieces,) = call(
        slices_kernel, [(16, 48, width)], [spots], [parts, wide, upper, lower_slices], 10**7
    )
    parts = exchange(pieces, CHIPS)
    mine, pieces = call(
        arrange_kernel, [(3 * separator, width), (32, 8, width)], [], [parts], 10**7
    )
    theirs = partner(mine, "k")
    low_rows = exchange(pieces, PLANE)

    (pieces,) = call(
        backward_kernel,
        [(8, 128, width)],
        [spots, front_ranks],
        [
            gains,
            low_rows,
            mine,
            theirs,
            flipped(inverse_root),
            inverse_upper,
            flipped(inverse_middle),
            inverse_lower,
            flipped(basis_upper),
            flipped(basis_middle),
            flipped(basis_lower),
            shared,
        ],
        3 * 10**9,
    )
    total = exchange(pieces, ("c",)).sum(axis=0)
    tops = total[:48].reshape(2, 24, width)
    tops = select(tops, d) + partner(select(tops, 1 - d), "d")
    (leaf_solution,) = call(
        last_kernel,
        [leaf_source.shape],
        [leaf_ranks],
        [total[96:], leaf_forward, leaf_inverse, flipped(leaf_basis)],
        10**9,
    )
    return (
        tops[None, None, :12],
        tops[None, None, 12:],
        total[None, None, 48:72],
        total[None, None, 72:96],
        leaf_solution,
    )


def solution(mesh):
    fine = Mesh(mesh.devices.reshape(2, 2, 4, 2, 2, 8), ROW + COL)
    tile = (ROW, COL)
    in_specs = (
        [P(*tile, None, None, None)] * 5
        + [P(ROW, None, None, None)] * 4
        + [P(*tile, None, None)]
        + [P(ROW, None, None, None, None, None)] * 3
        + [P(*tile, None, None, None)]
        + [P(ROW, None, None, None)] * 3
        + [P(*tile, None)]
        + [P(COL, None, None, None, None)] * 3
        + [P(*tile, None, None, None), P(), P(*tile)]
    )
    return jax.shard_map(
        body,
        mesh=fine,
        in_specs=tuple(in_specs),
        out_specs=(P(*tile, None, None),) * 5,
        check_vma=False,
    )
```

```python
import jax
import jax.numpy as jnp
from jax import lax
from jax.experimental import pallas as pl
from jax.experimental.pallas import tpu as pltpu
from jax.sharding import Mesh, PartitionSpec as P

precise = lax.Precision.HIGHEST

ROW = ("a", "e", "z", "k")
COL = ("d", "c")
CHIPS = ("a", "e", "z")
PLANE = ("k", "d", "c")


def exchange(pieces, axes):
    return lax.all_to_all(pieces, axes, 0, 0)


def partner(values, axis):
    return lax.ppermute(values, axis, [(0, 1), (1, 0)])


def turned(values):
    groups = []
    for at in range(0, values.shape[-1], 128):
        groups += [-values[:, at + 64 : at + 128], values[:, at : at + 64]]
    return jnp.concatenate(groups, axis=-1)


def halves(values):
    high = values.astype(jnp.bfloat16)
    return high, (values - high.astype(jnp.float32)).astype(jnp.bfloat16)


def dot(left, right, contract=1):
    left_high, left_low = halves(left)
    right_high, right_low = halves(right)

    def one(x, y):
        return lax.dot_general(
            x, y, (((contract,), (0,)), ((), ())), preferred_element_type=jnp.float32
        )

    return one(left_high, right_high) + (one(left_high, right_low) + one(left_low, right_high))


def times(real, imag, vector):
    return dot(real, vector) + dot(imag, turned(vector))


def times_back(real, imag, vector):
    return dot(real, vector, 0) + dot(imag, turned(vector), 0)


def cut(values, limit):
    rows = lax.broadcasted_iota(jnp.int32, values.shape, 0)
    return jnp.where(rows < limit, values, jnp.zeros_like(values))


def put_thin(target, row, part):
    nothing = jnp.zeros((2, 128), jnp.float32)
    for chip in range(16):
        slot = jnp.concatenate([part[6 * chip : 6 * chip + 6], nothing], axis=0)
        target[chip, row : row + 8] = slot


def leaf_kernel(ranks, forward, packs, inverse, source, basis, update, slots):
    inner = inverse.shape[-1]
    result = times(inverse[0, 0, 0], inverse[0, 0, 1], source[0, 0])
    forward[...] = result
    low = cut(times(basis[0, 0, 0], basis[0, 0, 1], result), ranks[0, 0])
    height = inner // 2
    places = lax.broadcasted_iota(jnp.int32, (height, slots.shape[-1]), 0)
    onehot = (places == slots[0]).astype(jnp.float32)
    flat = jnp.concatenate([update[0, 0, 0], update[0, 0, 1]], axis=0)
    spread_out = lax.dot_general(
        flat,
        onehot,
        (((1,), (1,)), ((), ())),
        precision=precise,
        preferred_element_type=jnp.float32,
    )
    half = low.shape[0]
    pack = jnp.concatenate(
        [
            low,
            spread_out[:, :128],
            jnp.concatenate([spread_out[:half, 128:], spread_out[half:, 128:]], axis=-1),
        ],
        axis=0,
    )
    for place in range(packs.shape[0]):
        packs[place] = pack


def apply_kernel(
    spots,
    keep,
    send,
    lows,
    inverse0,
    inverse1,
    inverse2,
    source0,
    source1,
    source2,
    update0,
    update1,
    update2,
    slots0,
    slots1,
    slots2,
    basis1,
    basis2,
):
    a, k, d = spots[0], spots[2], spots[3]
    results = []
    for inverse, source, update, slots, at in (
        (inverse0, source0, update0, slots0, 0),
        (inverse1, source1, update1, slots1, 0),
        (inverse2, source2, update2, slots2, d),
    ):
        right = source[0, at]
        height = right.shape[0]
        lists = slots[0, at]
        places = lax.broadcasted_iota(jnp.int32, (height, lists.shape[-1]), 0)
        spread_out = jnp.zeros((height, 128), jnp.float32)
        for child in range(2):
            onehot = (places == lists[child : child + 1]).astype(jnp.float32)
            real, imag = update[0, at, child, 0], update[0, at, child, 1]
            nothing = jnp.zeros_like(real)
            order = [real, nothing, imag, nothing] if child == 0 else [nothing, real, nothing, imag]
            spread_out += lax.dot_general(
                onehot,
                jnp.concatenate(order, axis=0),
                (((1,), (1,)), ((), ())),
                precision=precise,
                preferred_element_type=jnp.float32,
            )
        both = jnp.concatenate([right, spread_out], axis=-1)
        apply = times if inverse is inverse1 else times_back
        results.append(apply(inverse[0, 0, 0], inverse[0, 0, 1], both))
    low2 = times(basis2[0, a, 0], basis2[0, a, 1], results[2])
    low1 = times(basis1[0, a, 0], basis1[0, a, 1], results[1])
    lows[0] = low2[:, :128]
    lows[1] = low2[:, 128:]
    lows[2] = low1[:, :128]
    lows[3] = low1[:, 128:]

    def put(target, half):
        for side in range(2):
            for level, at in ((0, 0), (2, 8)):
                rows = results[level].shape[0] // 2
                part = results[level][half * rows : (half + 1) * rows, side * 128 : side * 128 + 128]
                target[at : at + 8, 24 * side : 24 * side + 24] = part.reshape(8, 24, 128)
            rows = results[1].shape[0] // 2
            part = results[1][half * rows : (half + 1) * rows, side * 128 : side * 128 + 128]
            row = 48 + 8 * side
            put_thin(target, row, part)

    for half in range(2):

        @pl.when(k == half)
        def _(half=half):
            put(keep, half)
            put(send, 1 - half)


def lower_kernel(spots, keep, send, rows, shared, lows, inverse, source, basis):
    a, e, k, d = spots[0], spots[1], spots[2], spots[3]
    low = shared[:, 0:32].reshape(256, 128)
    low_turned = turned(low)
    packs = shared[:, 96:128].reshape(256, 128)
    top = dot(shared[:, 32:64].reshape(256, 128), low, 0) + dot(
        shared[:, 64:96].reshape(256, 128), low_turned, 0
    )
    rest = dot(packs[:, :64], low, 0) + dot(packs[:, 64:], low_turned, 0)
    side = source[0, d] - jnp.concatenate([top, rest], axis=0)
    partial = times(inverse[0, 0, 0], inverse[0, 0, 1], side)
    front = 2 * a + e
    low3 = times(basis[0, front, 0], basis[0, front, 1], partial)
    rows[:, 0, :] = low3
    for at in range(4):
        rows[:, at + 1, :] = lows[at]
    for at in range(5, 8):
        rows[:, at, :] = jnp.zeros((32, 128), jnp.float32)
    count = partial.shape[0] // 2

    def put(target, half):
        put_thin(target, 0, partial[half * count : (half + 1) * count])

    for half in range(2):

        @pl.when(k == half)
        def _(half=half):
            put(keep, half)
            put(send, 1 - half)


def backward_kernel(
    spots,
    ranks,
    gains,
    lows,
    mine,
    theirs,
    inverse0,
    inverse1,
    inverse2,
    inverse3,
    basis1,
    basis2,
    basis3,
    shared,
    pieces,
):
    a, e, k, d = spots[0], spots[1], spots[2], spots[3]

    def gain_back(gain, low, child):
        both = times_back(gain[:, :64], gain[:, 64:], low)
        return jnp.where(child == 0, both[:32], both[32:])

    gain1 = jnp.where(a == 0, gains[:, 18, :], gains[:, 19, :])
    gain2 = jnp.where(
        a == 0,
        jnp.where(d == 0, gains[:, 12, :], gains[:, 13, :]),
        jnp.where(d == 0, gains[:, 14, :], gains[:, 15, :]),
    )
    back1 = cut(lows[:, 0, :], ranks[a])
    back2 = cut(lows[:, 1, :] - gain_back(gain1, back1, d), ranks[2 + 2 * a + d])
    back3 = cut(lows[:, 2, :] - gain_back(gain2, back2, e), ranks[6 + 4 * a + 2 * e + d])

    def whole(start, stop):
        left, right = mine[start:stop], theirs[start:stop]
        return jnp.concatenate(
            [jnp.where(k == 0, left, right), jnp.where(k == 0, right, left)], axis=0
        )

    front = 2 * a + e
    residuals = (
        whole(0, 192),
        whole(384, 480) - times_back(basis1[0, a, 0], basis1[0, a, 1], back1),
        whole(192, 384) - times_back(basis2[0, a, 0], basis2[0, a, 1], back2),
        whole(480, 576) - times_back(basis3[0, front, 0], basis3[0, front, 1], back3),
    )
    solved = [
        times(inverse0[0, 0, 0], inverse0[0, 0, 1], residuals[0]),
        times_back(inverse1[0, 0, 0], inverse1[0, 0, 1], residuals[1]),
        times(inverse2[0, 0, 0], inverse2[0, 0, 1], residuals[2]),
        times_back(inverse3[0, 0, 0], inverse3[0, 0, 1], residuals[3]),
    ]
    for level in range(2):
        for place in range(2):
            for to_c in range(8):
                at = 96 * place + 12 * to_c
                row = 24 * place + 12 * level
                pieces[to_c, row : row + 12] = solved[level][at : at + 12]
    pieces[:, 48:72] = solved[2].reshape(8, 24, 128)
    pieces[:, 72:96] = solved[3].reshape(8, 24, 128)
    lowest = solved[3]
    lowest_turned = turned(lowest)
    packs = shared[:, 96:128].reshape(256, 128)
    parts = (
        dot(shared[:, 32:64].reshape(256, 128), lowest[:128])
        + dot(shared[:, 64:96].reshape(256, 128), lowest_turned[:128])
        + dot(packs[:, :64], lowest[128:])
        + dot(packs[:, 64:], lowest_turned[128:])
    )
    pieces[:, 96:128] = parts.reshape(8, 32, 128)


def last_kernel(ranks, low, forward, inverse, basis, solved):
    back = cut(low[...], ranks[0, 0])
    rest = forward[...] - times_back(basis[0, 0, 0], basis[0, 0, 1], back)
    solved[0, 0] = times_back(inverse[0, 0, 0], inverse[0, 0, 1], rest)


def gather_kernel(parts, applied_keep, applied_got, lower_keep, lower_got, pieces):
    sums = []
    for place in range(2):
        total = jnp.zeros((8, 128), jnp.float32)
        for core in range(2):
            for at in range(8):
                total += parts[16 * core + 8 * place + at]
        sums.append(total)
    rows = [sums[place][row : row + 1] for row in range(3) for place in range(2)]
    rows += [sums[0][3:5] + sums[1][3:5]]
    tile = jnp.concatenate(rows, axis=0)
    for chip in range(16):
        pieces[chip, 0:8] = tile
        pieces[chip, 8:16] = lower_keep[chip] + lower_got[chip]
        pieces[chip, 16:80] = applied_keep[chip] + applied_got[chip]


def total_kernel(parts, pieces, sums, lower):
    tiles = []
    for at in range(4):
        total = parts[4 * at]
        for chip in range(1, 4):
            total += parts[4 * at + chip]
        tiles.append(total)
        lower[at] = total[8:16]
    upper = []
    for place in range(2):
        total = tiles[2 * place] + tiles[2 * place + 1]
        sums[place] = total[16:80]
        upper.append(total)
    rows = [tile[0:2] for tile in tiles]
    for start, stop in ((2, 4), (4, 6), (6, 7), (7, 8)):
        rows += [total[start:stop] for total in upper]
    rows += [jnp.zeros((4, 128), jnp.float32)]
    tile = jnp.concatenate(rows, axis=0)
    for place in range(32):
        pieces[place] = tile


def forward_kernel(spots, ranks, gains, sums, wide_out, upper_out, rows):
    a, d = spots[0], spots[3]
    coeffs3 = [cut(gains[:, at, :], ranks[6 + at]) for at in range(8)]
    pairs3 = [
        [jnp.concatenate([coeffs3[4 * x + y], coeffs3[4 * x + 2 + y]], axis=0) for y in range(2)]
        for x in range(2)
    ]

    def chain(total, gain, pair, limit):
        return cut(total - times(gain[:, :64], gain[:, 64:], pair), limit)

    pairs2 = []
    for x in range(2):
        both = [
            chain(
                gains[:, 8 + 2 * x + y, :],
                gains[:, 12 + 2 * x + y, :],
                pairs3[x][y],
                ranks[2 + 2 * x + y],
            )
            for y in range(2)
        ]
        pairs2.append(jnp.concatenate(both, axis=0))
    pair1 = jnp.concatenate(
        [chain(gains[:, 16 + x, :], gains[:, 18 + x, :], pairs2[x], ranks[x]) for x in range(2)],
        axis=0,
    )
    everything = sums[0, 0:48] + sums[1, 0:48]
    for x in range(2):
        below = jnp.where(a == 0, pair1, jnp.where(d == 0, pairs3[x][0], pairs3[x][1]))
        slices = jnp.where(a == 0, everything, sums[x, 0:48])
        gain = slices[24:48]
        result = slices[0:24] - times(gain[:, :64], gain[:, 64:], below)
        wide_out[x] = result
        low = times_back(gain[:, :64], gain[:, 64:], result)
        rows[:, 2 * x, :] = low[:32]
        rows[:, 2 * x + 1, :] = low[32:]
        gain = sums[x, 56:64]
        result = sums[x, 48:56] - times(gain[:, :64], gain[:, 64:], pairs2[x])
        upper_out[x] = result
        low = times_back(gain[:, :64], gain[:, 64:], result)
        rows[:, 4 + 2 * x, :] = low[:32]
        rows[:, 5 + 2 * x, :] = low[32:]


def slices_kernel(spots, parts, wide, upper, lower, pieces):
    a = spots[0]
    sums = []
    for place in range(2):
        total = jnp.zeros((8, 128), jnp.float32)
        for core in range(2):
            for at in range(8):
                total += parts[16 * core + 8 * place + at]
        sums.append(total)
    joined = sums[0] + sums[1]
    nothing = jnp.zeros((1, 128), jnp.float32)
    for to_a in range(2):
        for to_e in range(2):
            row = 2 * to_a + to_e
            tile = jnp.concatenate(
                [
                    jnp.where(a == 0, joined[to_a : to_a + 1], sums[0][row : row + 1]),
                    jnp.where(a == 0, nothing, sums[1][row : row + 1]),
                    joined[4 + 2 * to_a : 6 + 2 * to_a],
                ],
                axis=0,
            )
            tile = jnp.concatenate([upper[to_a][0:6], lower[row][0:6], tile], axis=0)
            for chip in range(4):
                place = 8 * to_a + 4 * to_e + chip
                pieces[place, 0:24] = wide[to_a]
                pieces[place, 24:40] = tile


def arrange_kernel(parts, mine, pieces):
    for chip in range(8):
        mine[24 * chip : 24 * chip + 24] = parts[chip, 0:24]
        mine[192 + 24 * chip : 216 + 24 * chip] = parts[8 + chip, 0:24]
    tails = [parts[chip, 24:40] for chip in range(16)]
    mine[384:480] = jnp.concatenate([tail[0:6] for tail in tails], axis=0)
    mine[480:576] = jnp.concatenate([tail[6:12] for tail in tails], axis=0)
    sums = []
    for place in range(2):
        total = tails[8 * place]
        for chip in range(1, 8):
            total += tails[8 * place + chip]
        sums.append(total[12:16])
    upper = sums[0] + sums[1]
    tail = jnp.zeros((5, 128), jnp.float32)
    for to_d in range(2):
        tile = jnp.concatenate(
            [sums[0][0:1], upper[2 + to_d : 3 + to_d], sums[1][to_d : to_d + 1], tail], axis=0
        )
        for core in range(2):
            for to_c in range(8):
                pieces[16 * core + 8 * to_d + to_c] = tile


def flipped(values):
    return jnp.swapaxes(values, -1, -2)


def call(kernel, shapes, scalars, arrays, flops, fetched=()):
    count = len(fetched)
    places = len(scalars[0]) if isinstance(scalars[0:1] and scalars[0], tuple) else 0
    before = len(scalars) + len(arrays)
    scalars = [*scalars[0], *scalars[1:]] if places else scalars

    def outer(*refs):
        if places:
            refs = (tuple(ref[0] for ref in refs[:places]),) + refs[places:]
        inputs, sources = refs[:before], refs[before : before + count]
        outputs = refs[before + count : before + count + len(shapes)]
        buffers = refs[before + count + len(shapes) :]
        if count:
            sems = buffers[-1]
            copies = [
                pltpu.make_async_copy(source, buffer, sems.at[at])
                for at, (source, buffer) in enumerate(zip(sources, buffers[:-1]))
            ]
            for copy in copies:
                copy.start()
            for copy in copies:
                copy.wait()
        kernel(*inputs, *outputs, *buffers[:count])

    scratch = [pltpu.VMEM(array.shape, array.dtype) for array in fetched]
    if count:
        scratch.append(pltpu.SemaphoreType.DMA((count,)))
    return pl.pallas_call(
        outer,
        out_shape=[jax.ShapeDtypeStruct(shape, jnp.float32) for shape in shapes],
        in_specs=[pl.BlockSpec(memory_space=pltpu.SMEM)] * len(scalars)
        + [pl.BlockSpec(memory_space=pltpu.VMEM)] * len(arrays)
        + [pl.BlockSpec(memory_space=pltpu.HBM)] * count,
        out_specs=[pl.BlockSpec(memory_space=pltpu.VMEM)] * len(shapes),
        scratch_shapes=scratch,
        compiler_params=pltpu.CompilerParams(vmem_limit_bytes=(60 if count else 24) * 2**20),
        cost_estimate=pl.CostEstimate(flops=flops, bytes_accessed=4 * 2**20, transcendentals=0),
    )(*scalars, *arrays, *fetched)


def select(array, position):
    return lax.dynamic_index_in_dim(array, position, 0, keepdims=False)


def body(
    inverse_root,
    inverse_upper,
    inverse_middle,
    inverse_lower,
    leaf_inverse,
    source_root,
    source_upper,
    source_middle,
    source_lower,
    leaf_source,
    update_root,
    update_upper,
    update_middle,
    leaf_update,
    slots_root,
    slots_upper,
    slots_middle,
    leaf_slots,
    basis_upper,
    basis_middle,
    basis_lower,
    leaf_basis,
    front_ranks,
    leaf_ranks,
):
    a, e, k, d = (lax.axis_index(name) for name in ("a", "e", "k", "d"))
    separator, width = source_root.shape[2:]
    rank = leaf_basis.shape[-1]
    spots = tuple(axis.astype(jnp.int32).reshape(1) for axis in (a, e, k, d))

    leaf_forward, packs = call(
        leaf_kernel,
        [leaf_source.shape[2:], (8, 128, width)],
        [leaf_ranks],
        [],
        10**9,
        [leaf_inverse, leaf_source, flipped(leaf_basis), flipped(leaf_update), leaf_slots],
    )
    shared = exchange(packs, ("c",))

    keep, send, lows = call(
        apply_kernel,
        [(16, 64, width), (16, 64, width), (4, rank, width)],
        [spots],
        [],
        4 * 10**9,
        [
            flipped(inverse_root),
            inverse_upper,
            flipped(inverse_middle),
            source_root,
            source_upper,
            source_middle,
            flipped(update_root),
            flipped(update_upper),
            flipped(update_middle),
            slots_root,
            slots_upper,
            slots_middle,
            flipped(basis_upper),
            flipped(basis_middle),
        ],
    )
    applied = (keep, partner(send, "k"))
    keep, send, rows = call(
        lower_kernel,
        [(16, 8, width), (16, 8, width), (rank, 8, width)],
        [spots],
        [],
        10**9,
        [shared, lows, inverse_lower, source_lower, flipped(basis_lower)],
    )
    lower = (keep, partner(send, "k"))

    parts = exchange(rows, PLANE)
    (pieces,) = call(gather_kernel, [(16, 80, width)], [], [parts, *applied, *lower], 10**7)
    parts = exchange(pieces, CHIPS)
    pieces, sums, lower_slices = call(
        total_kernel, [(32, 24, width), (2, 64, width), (4, 8, width)], [], [parts], 10**7
    )
    gains = exchange(pieces, PLANE)

    wide, upper, rows = call(
        forward_kernel,
        [(2, 24, width), (2, 8, width), (rank, 8, width)],
        [spots, front_ranks],
        [gains, sums],
        10**8,
    )
    parts = exchange(rows, PLANE)
    (pieces,) = call(
        slices_kernel, [(16, 40, width)], [spots], [parts, wide, upper, lower_slices], 10**7
    )
    parts = exchange(pieces, CHIPS)
    mine, pieces = call(
        arrange_kernel, [(3 * separator, width), (32, 8, width)], [], [parts], 10**7
    )
    theirs = partner(mine, "k")
    low_rows = exchange(pieces, PLANE)

    (pieces,) = call(
        backward_kernel,
        [(8, 128, width)],
        [spots, front_ranks],
        [
            gains,
            low_rows,
            mine,
            theirs,
            flipped(inverse_root),
            inverse_upper,
            flipped(inverse_middle),
            inverse_lower,
            flipped(basis_upper),
            flipped(basis_middle),
            flipped(basis_lower),
            shared,
        ],
        3 * 10**9,
    )
    total = exchange(pieces, ("c",)).sum(axis=0)
    tops = total[:48].reshape(2, 24, width)
    tops = select(tops, d) + partner(select(tops, 1 - d), "d")
    (leaf_solution,) = call(
        last_kernel,
        [leaf_source.shape],
        [leaf_ranks],
        [total[96:], leaf_forward, leaf_inverse, flipped(leaf_basis)],
        10**9,
    )
    return (
        tops[None, None, :12],
        tops[None, None, 12:],
        total[None, None, 48:72],
        total[None, None, 72:96],
        leaf_solution,
    )


def solution(mesh):
    fine = Mesh(mesh.devices.reshape(2, 2, 4, 2, 2, 8), ROW + COL)
    tile = (ROW, COL)
    in_specs = (
        [P(*tile, None, None, None)] * 5
        + [P(ROW, None, None, None)] * 4
        + [P(*tile, None, None)]
        + [P(ROW, None, None, None, None, None)] * 3
        + [P(*tile, None, None, None)]
        + [P(ROW, None, None, None)] * 3
        + [P(*tile, None)]
        + [P(COL, None, None, None, None)] * 3
        + [P(*tile, None, None, None), P(), P(*tile)]
    )
    return jax.shard_map(
        body,
        mesh=fine,
        in_specs=tuple(in_specs),
        out_specs=(P(*tile, None, None),) * 5,
        check_vma=False,
    )
```

```python
import jax
import jax.numpy as jnp
from jax import lax
from jax.experimental import pallas as pl
from jax.experimental.pallas import tpu as pltpu
from jax.sharding import Mesh, PartitionSpec as P

precise = lax.Precision.HIGHEST

ROW = ("a", "e", "z", "k")
COL = ("d", "c")
CHIPS = ("a", "e", "z")
PLANE = ("k", "d", "c")


def exchange(pieces, axes):
    return lax.all_to_all(pieces, axes, 0, 0)


def partner(values, axis):
    return lax.ppermute(values, axis, [(0, 1), (1, 0)])


def turned(values):
    groups = []
    for at in range(0, values.shape[-1], 128):
        groups += [-values[:, at + 64 : at + 128], values[:, at : at + 64]]
    return jnp.concatenate(groups, axis=-1)


def halves(values):
    high = values.astype(jnp.bfloat16)
    return high, (values - high.astype(jnp.float32)).astype(jnp.bfloat16)


def dot(left, right, contract=1):
    left_high, left_low = halves(left)
    right_high, right_low = halves(right)

    def one(x, y):
        return lax.dot_general(
            x, y, (((contract,), (0,)), ((), ())), preferred_element_type=jnp.float32
        )

    return one(left_high, right_high) + (one(left_high, right_low) + one(left_low, right_high))


def times(real, imag, vector):
    return dot(real, vector) + dot(imag, turned(vector))


def times_back(real, imag, vector):
    return dot(real, vector, 0) + dot(imag, turned(vector), 0)


def cut(values, limit):
    rows = lax.broadcasted_iota(jnp.int32, values.shape, 0)
    return jnp.where(rows < limit, values, jnp.zeros_like(values))


def put_thin(target, row, part):
    nothing = jnp.zeros((2, 128), jnp.float32)
    for chip in range(16):
        slot = jnp.concatenate([part[6 * chip : 6 * chip + 6], nothing], axis=0)
        target[chip, row : row + 8] = slot


def leaf_kernel(ranks, forward, packs, inverse, source, basis, update, slots):
    inner = inverse.shape[-1]
    result = times(inverse[0, 0, 0], inverse[0, 0, 1], source[0, 0])
    forward[...] = result
    low = cut(times(basis[0, 0, 0], basis[0, 0, 1], result), ranks[0, 0])
    height = inner // 2
    places = lax.broadcasted_iota(jnp.int32, (height, slots.shape[-1]), 0)
    onehot = (places == slots[0]).astype(jnp.float32)
    flat = jnp.concatenate([update[0, 0, 0], update[0, 0, 1]], axis=0)
    spread_out = lax.dot_general(
        flat,
        onehot,
        (((1,), (1,)), ((), ())),
        precision=precise,
        preferred_element_type=jnp.float32,
    )
    half = low.shape[0]
    pack = jnp.concatenate(
        [
            low,
            spread_out[:, :128],
            jnp.concatenate([spread_out[:half, 128:], spread_out[half:, 128:]], axis=-1),
        ],
        axis=0,
    )
    for place in range(packs.shape[0]):
        packs[place] = pack


def apply_kernel(
    spots,
    keep,
    send,
    lows,
    inverse0,
    inverse1,
    inverse2,
    source0,
    source1,
    source2,
    update0,
    update1,
    update2,
    slots0,
    slots1,
    slots2,
    basis1,
    basis2,
):
    a, k, d = spots[0], spots[2], spots[3]
    results = []
    for inverse, source, update, slots, at in (
        (inverse0, source0, update0, slots0, 0),
        (inverse1, source1, update1, slots1, 0),
        (inverse2, source2, update2, slots2, d),
    ):
        right = source[0, at]
        height = right.shape[0]
        lists = slots[0, at]
        places = lax.broadcasted_iota(jnp.int32, (height, lists.shape[-1]), 0)
        spread_out = jnp.zeros((height, 128), jnp.float32)
        for child in range(2):
            onehot = (places == lists[child : child + 1]).astype(jnp.float32)
            real, imag = update[0, at, child, 0], update[0, at, child, 1]
            nothing = jnp.zeros_like(real)
            order = [real, nothing, imag, nothing] if child == 0 else [nothing, real, nothing, imag]
            spread_out += lax.dot_general(
                onehot,
                jnp.concatenate(order, axis=0),
                (((1,), (1,)), ((), ())),
                precision=precise,
                preferred_element_type=jnp.float32,
            )
        both = jnp.concatenate([right, spread_out], axis=-1)
        apply = times if inverse is inverse1 else times_back
        results.append(apply(inverse[0, 0, 0], inverse[0, 0, 1], both))
    low2 = times(basis2[0, a, 0], basis2[0, a, 1], results[2])
    low1 = times(basis1[0, a, 0], basis1[0, a, 1], results[1])
    lows[0] = low2[:, :128]
    lows[1] = low2[:, 128:]
    lows[2] = low1[:, :128]
    lows[3] = low1[:, 128:]

    def put(target, half):
        for side in range(2):
            for level, at in ((0, 0), (2, 8)):
                rows = results[level].shape[0] // 2
                part = results[level][half * rows : (half + 1) * rows, side * 128 : side * 128 + 128]
                target[at : at + 8, 24 * side : 24 * side + 24] = part.reshape(8, 24, 128)
            rows = results[1].shape[0] // 2
            part = results[1][half * rows : (half + 1) * rows, side * 128 : side * 128 + 128]
            row = 48 + 8 * side
            put_thin(target, row, part)

    for half in range(2):

        @pl.when(k == half)
        def _(half=half):
            put(keep, half)
            put(send, 1 - half)


def lower_kernel(spots, keep, send, rows, shared, lows, inverse, source, basis):
    a, e, k, d = spots[0], spots[1], spots[2], spots[3]
    low = shared[:, 0:32].reshape(256, 128)
    low_turned = turned(low)
    packs = shared[:, 96:128].reshape(256, 128)
    top = dot(shared[:, 32:64].reshape(256, 128), low, 0) + dot(
        shared[:, 64:96].reshape(256, 128), low_turned, 0
    )
    rest = dot(packs[:, :64], low, 0) + dot(packs[:, 64:], low_turned, 0)
    side = source[0, d] - jnp.concatenate([top, rest], axis=0)
    partial = times(inverse[0, 0, 0], inverse[0, 0, 1], side)
    front = 2 * a + e
    low3 = times(basis[0, front, 0], basis[0, front, 1], partial)
    rows[:, 0, :] = low3
    for at in range(4):
        rows[:, at + 1, :] = lows[at]
    for at in range(5, 8):
        rows[:, at, :] = jnp.zeros((32, 128), jnp.float32)
    count = partial.shape[0] // 2

    def put(target, half):
        put_thin(target, 0, partial[half * count : (half + 1) * count])

    for half in range(2):

        @pl.when(k == half)
        def _(half=half):
            put(keep, half)
            put(send, 1 - half)


def backward_kernel(
    spots,
    ranks,
    gains,
    belows,
    lows,
    mine,
    theirs,
    inverse0,
    inverse1,
    inverse2,
    inverse3,
    basis1,
    basis2,
    basis3,
    shared,
    pieces,
):
    a, e, k, d = spots[0], spots[1], spots[2], spots[3]

    def gain_back(gain, low, child):
        both = times_back(gain[:, :64], gain[:, 64:], low)
        return jnp.where(child == 0, both[:32], both[32:])

    gain1 = jnp.where(a == 0, gains[:, 18, :], gains[:, 19, :])
    gain2 = jnp.where(
        a == 0,
        jnp.where(d == 0, gains[:, 12, :], gains[:, 13, :]),
        jnp.where(d == 0, gains[:, 14, :], gains[:, 15, :]),
    )

    def upward(level):
        square = lows[:, 2 * level + 1, :]
        return lows[:, 2 * level, :] - times(square[:, :64], square[:, 64:], belows[level])

    back1 = cut(upward(0), ranks[a])
    back2 = cut(upward(1) - gain_back(gain1, back1, d), ranks[2 + 2 * a + d])
    back3 = cut(upward(2) - gain_back(gain2, back2, e), ranks[6 + 4 * a + 2 * e + d])

    def whole(start, stop):
        left, right = mine[start:stop], theirs[start:stop]
        return jnp.concatenate(
            [jnp.where(k == 0, left, right), jnp.where(k == 0, right, left)], axis=0
        )

    front = 2 * a + e
    residuals = (
        whole(0, 192),
        whole(384, 480) - times_back(basis1[0, a, 0], basis1[0, a, 1], back1),
        whole(192, 384) - times_back(basis2[0, a, 0], basis2[0, a, 1], back2),
        whole(480, 576) - times_back(basis3[0, front, 0], basis3[0, front, 1], back3),
    )
    solved = [
        times(inverse0[0, 0, 0], inverse0[0, 0, 1], residuals[0]),
        times_back(inverse1[0, 0, 0], inverse1[0, 0, 1], residuals[1]),
        times(inverse2[0, 0, 0], inverse2[0, 0, 1], residuals[2]),
        times_back(inverse3[0, 0, 0], inverse3[0, 0, 1], residuals[3]),
    ]
    for level in range(2):
        for place in range(2):
            for to_c in range(8):
                at = 96 * place + 12 * to_c
                row = 24 * place + 12 * level
                pieces[to_c, row : row + 12] = solved[level][at : at + 12]
    pieces[:, 48:72] = solved[2].reshape(8, 24, 128)
    pieces[:, 72:96] = solved[3].reshape(8, 24, 128)
    lowest = solved[3]
    lowest_turned = turned(lowest)
    packs = shared[:, 96:128].reshape(256, 128)
    parts = (
        dot(shared[:, 32:64].reshape(256, 128), lowest[:128])
        + dot(shared[:, 64:96].reshape(256, 128), lowest_turned[:128])
        + dot(packs[:, :64], lowest[128:])
        + dot(packs[:, 64:], lowest_turned[128:])
    )
    pieces[:, 96:128] = parts.reshape(8, 32, 128)


def last_kernel(ranks, low, forward, inverse, basis, solved):
    back = cut(low[...], ranks[0, 0])
    rest = forward[...] - times_back(basis[0, 0, 0], basis[0, 0, 1], back)
    solved[0, 0] = times_back(inverse[0, 0, 0], inverse[0, 0, 1], rest)


def gather_kernel(parts, applied_keep, applied_got, lower_keep, lower_got, pieces):
    sums = []
    for place in range(2):
        total = jnp.zeros((8, 128), jnp.float32)
        for core in range(2):
            for at in range(8):
                total += parts[16 * core + 8 * place + at]
        sums.append(total)
    rows = [sums[place][row : row + 1] for row in range(3) for place in range(2)]
    rows += [sums[0][3:5] + sums[1][3:5]]
    tile = jnp.concatenate(rows, axis=0)
    for chip in range(16):
        pieces[chip, 0:8] = tile
        pieces[chip, 8:16] = lower_keep[chip] + lower_got[chip]
        pieces[chip, 16:80] = applied_keep[chip] + applied_got[chip]


def total_kernel(spots, parts, pieces, sums, lower):
    a = spots[0]
    tiles = []
    for at in range(4):
        total = parts[4 * at]
        for chip in range(1, 4):
            total += parts[4 * at + chip]
        tiles.append(total)
        lower[at] = total[8:16]
    upper = []
    for place in range(2):
        total = tiles[2 * place] + tiles[2 * place + 1]
        sums[place] = total[16:80]
        upper.append(total)
    rows = [tile[0:2] for tile in tiles]
    for start, stop in ((2, 4), (4, 6), (6, 7), (7, 8)):
        rows += [total[start:stop] for total in upper]
    rows += [jnp.zeros((4, 128), jnp.float32)]
    tile = jnp.concatenate(rows, axis=0)
    for place in range(32):
        pieces[place, 0:24] = tile
    everything = upper[0][16:64] + upper[1][16:64]
    for x in range(2):
        wide = jnp.where(a == 0, everything, upper[x][16:64])
        thin = upper[x][64:80]
        for at, slices in ((24, wide), (32, thin)):
            count = slices.shape[0] // 2
            gain = slices[count:]
            both = jnp.concatenate([slices[:count], gain], axis=-1)
            low = times_back(gain[:, :64], gain[:, 64:], both)
            for child in range(2):
                row = at + 4 * x + 2 * child
                pieces[:, row, :] = low[32 * child : 32 * child + 32, :128]
                pieces[:, row + 1, :] = low[32 * child : 32 * child + 32, 128:]


def forward_kernel(spots, ranks, gains, sums, lower, pieces, belows):
    a, d = spots[0], spots[3]
    coeffs3 = [cut(gains[:, at, :], ranks[6 + at]) for at in range(8)]
    pairs3 = [
        [jnp.concatenate([coeffs3[4 * x + y], coeffs3[4 * x + 2 + y]], axis=0) for y in range(2)]
        for x in range(2)
    ]

    def chain(total, gain, pair, limit):
        return cut(total - times(gain[:, :64], gain[:, 64:], pair), limit)

    pairs2 = []
    for x in range(2):
        both = [
            chain(
                gains[:, 8 + 2 * x + y, :],
                gains[:, 12 + 2 * x + y, :],
                pairs3[x][y],
                ranks[2 + 2 * x + y],
            )
            for y in range(2)
        ]
        pairs2.append(jnp.concatenate(both, axis=0))
    pair1 = jnp.concatenate(
        [chain(gains[:, 16 + x, :], gains[:, 18 + x, :], pairs2[x], ranks[x]) for x in range(2)],
        axis=0,
    )
    belows[0] = pair1
    belows[1] = jnp.where(a == 0, pairs2[0], pairs2[1])
    belows[2] = jnp.where(
        a == 0,
        jnp.where(d == 0, pairs3[0][0], pairs3[0][1]),
        jnp.where(d == 0, pairs3[1][0], pairs3[1][1]),
    )
    everything = sums[0, 0:48] + sums[1, 0:48]
    wide, upper = [], []
    for x in range(2):
        below = jnp.where(a == 0, pair1, jnp.where(d == 0, pairs3[x][0], pairs3[x][1]))
        slices = jnp.where(a == 0, everything, sums[x, 0:48])
        gain = slices[24:48]
        wide.append(slices[0:24] - times(gain[:, :64], gain[:, 64:], below))
        gain = sums[x, 56:64]
        upper.append(sums[x, 48:56] - times(gain[:, :64], gain[:, 64:], pairs2[x]))
    totals = []
    for place in range(2):
        total = jnp.zeros((16, 128), jnp.float32)
        for core in range(2):
            for at in range(8):
                total += gains[16 * core + 8 * place + at, 24:40]
        totals.append(total)
    joined = totals[0] + totals[1]
    nothing = jnp.zeros((2, 128), jnp.float32)
    tail = jnp.zeros((4, 128), jnp.float32)
    for to_a in range(2):
        for to_e in range(2):
            row = 4 * to_a + 2 * to_e
            tile = jnp.concatenate(
                [
                    upper[to_a][0:6],
                    lower[2 * to_a + to_e][0:6],
                    jnp.where(a == 0, joined[2 * to_a : 2 * to_a + 2], totals[0][row : row + 2]),
                    jnp.where(a == 0, nothing, totals[1][row : row + 2]),
                    joined[8 + 4 * to_a : 12 + 4 * to_a],
                    tail,
                ],
                axis=0,
            )
            for chip in range(4):
                place = 8 * to_a + 4 * to_e + chip
                pieces[place, 0:24] = wide[to_a]
                pieces[place, 24:48] = tile


def arrange_kernel(parts, mine, pieces):
    for chip in range(8):
        mine[24 * chip : 24 * chip + 24] = parts[chip, 0:24]
        mine[192 + 24 * chip : 216 + 24 * chip] = parts[8 + chip, 0:24]
    tails = [parts[chip, 24:48] for chip in range(16)]
    mine[384:480] = jnp.concatenate([tail[0:6] for tail in tails], axis=0)
    mine[480:576] = jnp.concatenate([tail[6:12] for tail in tails], axis=0)
    sums = []
    for place in range(2):
        total = tails[8 * place]
        for chip in range(1, 8):
            total += tails[8 * place + chip]
        sums.append(total[12:20])
    upper = sums[0] + sums[1]
    tail = jnp.zeros((2, 128), jnp.float32)
    for to_d in range(2):
        row = 2 * to_d
        tile = jnp.concatenate(
            [sums[0][0:2], upper[4 + row : 6 + row], sums[1][row : row + 2], tail], axis=0
        )
        for core in range(2):
            for to_c in range(8):
                pieces[16 * core + 8 * to_d + to_c] = tile


def flipped(values):
    return jnp.swapaxes(values, -1, -2)


def call(kernel, shapes, scalars, arrays, flops, fetched=()):
    count = len(fetched)
    places = len(scalars[0]) if isinstance(scalars[0:1] and scalars[0], tuple) else 0
    before = len(scalars) + len(arrays)
    scalars = [*scalars[0], *scalars[1:]] if places else scalars

    def outer(*refs):
        if places:
            refs = (tuple(ref[0] for ref in refs[:places]),) + refs[places:]
        inputs, sources = refs[:before], refs[before : before + count]
        outputs = refs[before + count : before + count + len(shapes)]
        buffers = refs[before + count + len(shapes) :]
        if count:
            sems = buffers[-1]
            copies = [
                pltpu.make_async_copy(source, buffer, sems.at[at])
                for at, (source, buffer) in enumerate(zip(sources, buffers[:-1]))
            ]
            for copy in copies:
                copy.start()
            for copy in copies:
                copy.wait()
        kernel(*inputs, *outputs, *buffers[:count])

    scratch = [pltpu.VMEM(array.shape, array.dtype) for array in fetched]
    if count:
        scratch.append(pltpu.SemaphoreType.DMA((count,)))
    return pl.pallas_call(
        outer,
        out_shape=[jax.ShapeDtypeStruct(shape, jnp.float32) for shape in shapes],
        in_specs=[pl.BlockSpec(memory_space=pltpu.SMEM)] * len(scalars)
        + [pl.BlockSpec(memory_space=pltpu.VMEM)] * len(arrays)
        + [pl.BlockSpec(memory_space=pltpu.HBM)] * count,
        out_specs=[pl.BlockSpec(memory_space=pltpu.VMEM)] * len(shapes),
        scratch_shapes=scratch,
        compiler_params=pltpu.CompilerParams(vmem_limit_bytes=(60 if count else 24) * 2**20),
        cost_estimate=pl.CostEstimate(flops=flops, bytes_accessed=4 * 2**20, transcendentals=0),
    )(*scalars, *arrays, *fetched)


def select(array, position):
    return lax.dynamic_index_in_dim(array, position, 0, keepdims=False)


def body(
    inverse_root,
    inverse_upper,
    inverse_middle,
    inverse_lower,
    leaf_inverse,
    source_root,
    source_upper,
    source_middle,
    source_lower,
    leaf_source,
    update_root,
    update_upper,
    update_middle,
    leaf_update,
    slots_root,
    slots_upper,
    slots_middle,
    leaf_slots,
    basis_upper,
    basis_middle,
    basis_lower,
    leaf_basis,
    front_ranks,
    leaf_ranks,
):
    a, e, k, d = (lax.axis_index(name) for name in ("a", "e", "k", "d"))
    separator, width = source_root.shape[2:]
    rank = leaf_basis.shape[-1]
    spots = tuple(axis.astype(jnp.int32).reshape(1) for axis in (a, e, k, d))

    leaf_forward, packs = call(
        leaf_kernel,
        [leaf_source.shape[2:], (8, 128, width)],
        [leaf_ranks],
        [],
        10**9,
        [leaf_inverse, leaf_source, flipped(leaf_basis), flipped(leaf_update), leaf_slots],
    )
    shared = exchange(packs, ("c",))

    keep, send, lows = call(
        apply_kernel,
        [(16, 64, width), (16, 64, width), (4, rank, width)],
        [spots],
        [],
        4 * 10**9,
        [
            flipped(inverse_root),
            inverse_upper,
            flipped(inverse_middle),
            source_root,
            source_upper,
            source_middle,
            flipped(update_root),
            flipped(update_upper),
            flipped(update_middle),
            slots_root,
            slots_upper,
            slots_middle,
            flipped(basis_upper),
            flipped(basis_middle),
        ],
    )
    applied = (keep, partner(send, "k"))
    keep, send, rows = call(
        lower_kernel,
        [(16, 8, width), (16, 8, width), (rank, 8, width)],
        [spots],
        [],
        10**9,
        [shared, lows, inverse_lower, source_lower, flipped(basis_lower)],
    )
    lower = (keep, partner(send, "k"))

    parts = exchange(rows, PLANE)
    (pieces,) = call(gather_kernel, [(16, 80, width)], [], [parts, *applied, *lower], 10**7)
    parts = exchange(pieces, CHIPS)
    pieces, sums, lower_slices = call(
        total_kernel, [(32, 40, width), (2, 64, width), (4, 8, width)], [spots], [parts], 10**7
    )
    gains = exchange(pieces, PLANE)

    pieces, belows = call(
        forward_kernel,
        [(16, 48, width), (3, 2 * rank, width)],
        [spots, front_ranks],
        [gains, sums, lower_slices],
        10**8,
    )
    parts = exchange(pieces, CHIPS)
    mine, pieces = call(
        arrange_kernel, [(3 * separator, width), (32, 8, width)], [], [parts], 10**7
    )
    theirs = partner(mine, "k")
    low_rows = exchange(pieces, PLANE)

    (pieces,) = call(
        backward_kernel,
        [(8, 128, width)],
        [spots, front_ranks],
        [
            gains,
            belows,
            low_rows,
            mine,
            theirs,
            flipped(inverse_root),
            inverse_upper,
            flipped(inverse_middle),
            inverse_lower,
            flipped(basis_upper),
            flipped(basis_middle),
            flipped(basis_lower),
            shared,
        ],
        3 * 10**9,
    )
    total = exchange(pieces, ("c",)).sum(axis=0)
    tops = total[:48].reshape(2, 24, width)
    tops = select(tops, d) + partner(select(tops, 1 - d), "d")
    (leaf_solution,) = call(
        last_kernel,
        [leaf_source.shape],
        [leaf_ranks],
        [total[96:], leaf_forward, leaf_inverse, flipped(leaf_basis)],
        10**9,
    )
    return (
        tops[None, None, :12],
        tops[None, None, 12:],
        total[None, None, 48:72],
        total[None, None, 72:96],
        leaf_solution,
    )


def solution(mesh):
    fine = Mesh(mesh.devices.reshape(2, 2, 4, 2, 2, 8), ROW + COL)
    tile = (ROW, COL)
    in_specs = (
        [P(*tile, None, None, None)] * 5
        + [P(ROW, None, None, None)] * 4
        + [P(*tile, None, None)]
        + [P(ROW, None, None, None, None, None)] * 3
        + [P(*tile, None, None, None)]
        + [P(ROW, None, None, None)] * 3
        + [P(*tile, None)]
        + [P(COL, None, None, None, None)] * 3
        + [P(*tile, None, None, None), P(), P(*tile)]
    )
    return jax.shard_map(
        body,
        mesh=fine,
        in_specs=tuple(in_specs),
        out_specs=(P(*tile, None, None),) * 5,
        check_vma=False,
    )
```

```python
import jax
import jax.numpy as jnp
from jax import lax
from jax.experimental import pallas as pl
from jax.experimental.pallas import tpu as pltpu
from jax.sharding import Mesh, PartitionSpec as P

ROW = ("a", "e", "z", "k")
COL = ("d", "c")
CHIPS = ("a", "e", "z")
PLANE = ("k", "d", "c")


def exchange(pieces, axes):
    return lax.all_to_all(pieces, axes, 0, 0)


def partner(values, axis):
    return lax.ppermute(values, axis, [(0, 1), (1, 0)])


def turned(values):
    groups = []
    for at in range(0, values.shape[-1], 128):
        groups += [-values[:, at + 64 : at + 128], values[:, at : at + 64]]
    return jnp.concatenate(groups, axis=-1)


def halves(values):
    high = values.astype(jnp.bfloat16)
    return high, (values - high.astype(jnp.float32)).astype(jnp.bfloat16)


def dot(left, right, contract=1):
    left_high, left_low = halves(left)
    right_high, right_low = halves(right)

    def one(x, y):
        return lax.dot_general(
            x, y, (((contract,), (0,)), ((), ())), preferred_element_type=jnp.float32
        )

    return one(left_high, right_high) + (one(left_high, right_low) + one(left_low, right_high))


def placed(values, onehot, rows):
    def one(part):
        left, right = (onehot, part) if rows else (part, onehot)
        return lax.dot_general(
            left, right, (((1,), (1,)), ((), ())), preferred_element_type=jnp.float32
        )

    high, low = halves(values)
    return one(high) + one(low)


def times(real, imag, vector):
    return dot(real, vector) + dot(imag, turned(vector))


def times_back(real, imag, vector):
    return dot(real, vector, 0) + dot(imag, turned(vector), 0)


def cut(values, limit):
    rows = lax.broadcasted_iota(jnp.int32, values.shape, 0)
    return jnp.where(rows < limit, values, jnp.zeros_like(values))


def put_thin(target, row, part):
    nothing = jnp.zeros((2, 128), jnp.float32)
    for chip in range(16):
        slot = jnp.concatenate([part[6 * chip : 6 * chip + 6], nothing], axis=0)
        target[chip, row : row + 8] = slot


def leaf_kernel(ranks, forward, packs, inverse, source, basis, update, slots):
    inner = inverse.shape[-1]
    result = times(inverse[0, 0, 0], inverse[0, 0, 1], source[0, 0])
    forward[...] = result
    low = cut(times(basis[0, 0, 0], basis[0, 0, 1], result), ranks[0, 0])
    height = inner // 2
    places = lax.broadcasted_iota(jnp.int32, (height, slots.shape[-1]), 0)
    onehot = (places == slots[0]).astype(jnp.bfloat16)
    flat = jnp.concatenate([update[0, 0, 0], update[0, 0, 1]], axis=0)
    spread_out = placed(flat, onehot, False)
    half = low.shape[0]
    pack = jnp.concatenate(
        [
            low,
            spread_out[:, :128],
            jnp.concatenate([spread_out[:half, 128:], spread_out[half:, 128:]], axis=-1),
        ],
        axis=0,
    )
    for place in range(packs.shape[0]):
        packs[place] = pack


def apply_kernel(
    spots,
    keep,
    send,
    lows,
    inverse0,
    inverse1,
    inverse2,
    source0,
    source1,
    source2,
    update0,
    update1,
    update2,
    slots0,
    slots1,
    slots2,
    basis1,
    basis2,
):
    a, k, d = spots[0], spots[2], spots[3]
    results = []
    for inverse, source, update, slots, at in (
        (inverse0, source0, update0, slots0, 0),
        (inverse1, source1, update1, slots1, 0),
        (inverse2, source2, update2, slots2, d),
    ):
        right = source[0, at]
        height = right.shape[0]
        lists = slots[0, at]
        places = lax.broadcasted_iota(jnp.int32, (height, lists.shape[-1]), 0)
        spread_out = jnp.zeros((height, 128), jnp.float32)
        for child in range(2):
            onehot = (places == lists[child : child + 1]).astype(jnp.bfloat16)
            real, imag = update[0, at, child, 0], update[0, at, child, 1]
            nothing = jnp.zeros_like(real)
            order = [real, nothing, imag, nothing] if child == 0 else [nothing, real, nothing, imag]
            spread_out += placed(jnp.concatenate(order, axis=0), onehot, True)
        both = jnp.concatenate([right, spread_out], axis=-1)
        apply = times if inverse is inverse1 else times_back
        results.append(apply(inverse[0, 0, 0], inverse[0, 0, 1], both))
    low2 = times(basis2[0, a, 0], basis2[0, a, 1], results[2])
    low1 = times(basis1[0, a, 0], basis1[0, a, 1], results[1])
    lows[0] = low2[:, :128]
    lows[1] = low2[:, 128:]
    lows[2] = low1[:, :128]
    lows[3] = low1[:, 128:]

    def put(target, half):
        for side in range(2):
            for level, at in ((0, 0), (2, 8)):
                rows = results[level].shape[0] // 2
                part = results[level][half * rows : (half + 1) * rows, side * 128 : side * 128 + 128]
                target[at : at + 8, 24 * side : 24 * side + 24] = part.reshape(8, 24, 128)
            rows = results[1].shape[0] // 2
            part = results[1][half * rows : (half + 1) * rows, side * 128 : side * 128 + 128]
            row = 48 + 8 * side
            put_thin(target, row, part)

    for half in range(2):

        @pl.when(k == half)
        def _(half=half):
            put(keep, half)
            put(send, 1 - half)


def lower_kernel(spots, keep, send, rows, shared, lows, inverse, source, basis):
    a, e, k, d = spots[0], spots[1], spots[2], spots[3]
    low = shared[:, 0:32].reshape(256, 128)
    low_turned = turned(low)
    packs = shared[:, 96:128].reshape(256, 128)
    top = dot(shared[:, 32:64].reshape(256, 128), low, 0) + dot(
        shared[:, 64:96].reshape(256, 128), low_turned, 0
    )
    rest = dot(packs[:, :64], low, 0) + dot(packs[:, 64:], low_turned, 0)
    side = source[0, d] - jnp.concatenate([top, rest], axis=0)
    partial = times(inverse[0, 0, 0], inverse[0, 0, 1], side)
    front = 2 * a + e
    low3 = times(basis[0, front, 0], basis[0, front, 1], partial)
    rows[:, 0, :] = low3
    for at in range(4):
        rows[:, at + 1, :] = lows[at]
    for at in range(5, 8):
        rows[:, at, :] = jnp.zeros((32, 128), jnp.float32)
    count = partial.shape[0] // 2

    def put(target, half):
        put_thin(target, 0, partial[half * count : (half + 1) * count])

    for half in range(2):

        @pl.when(k == half)
        def _(half=half):
            put(keep, half)
            put(send, 1 - half)


def backward_kernel(
    spots,
    ranks,
    gains,
    belows,
    lows,
    mine,
    theirs,
    inverse0,
    inverse1,
    inverse2,
    inverse3,
    basis1,
    basis2,
    basis3,
    shared,
    pieces,
):
    a, e, k, d = spots[0], spots[1], spots[2], spots[3]

    def gain_back(gain, low, child):
        both = times_back(gain[:, :64], gain[:, 64:], low)
        return jnp.where(child == 0, both[:32], both[32:])

    gain1 = jnp.where(a == 0, gains[:, 18, :], gains[:, 19, :])
    gain2 = jnp.where(
        a == 0,
        jnp.where(d == 0, gains[:, 12, :], gains[:, 13, :]),
        jnp.where(d == 0, gains[:, 14, :], gains[:, 15, :]),
    )

    def upward(level):
        square = lows[:, 2 * level + 1, :]
        return lows[:, 2 * level, :] - times(square[:, :64], square[:, 64:], belows[level])

    back1 = cut(upward(0), ranks[a])
    back2 = cut(upward(1) - gain_back(gain1, back1, d), ranks[2 + 2 * a + d])
    back3 = cut(upward(2) - gain_back(gain2, back2, e), ranks[6 + 4 * a + 2 * e + d])

    def whole(start, stop):
        left, right = mine[start:stop], theirs[start:stop]
        return jnp.concatenate(
            [jnp.where(k == 0, left, right), jnp.where(k == 0, right, left)], axis=0
        )

    front = 2 * a + e
    residuals = (
        whole(0, 192),
        whole(384, 480) - times_back(basis1[0, a, 0], basis1[0, a, 1], back1),
        whole(192, 384) - times_back(basis2[0, a, 0], basis2[0, a, 1], back2),
        whole(480, 576) - times_back(basis3[0, front, 0], basis3[0, front, 1], back3),
    )
    solved = [
        times(inverse0[0, 0, 0], inverse0[0, 0, 1], residuals[0]),
        times_back(inverse1[0, 0, 0], inverse1[0, 0, 1], residuals[1]),
        times(inverse2[0, 0, 0], inverse2[0, 0, 1], residuals[2]),
        times_back(inverse3[0, 0, 0], inverse3[0, 0, 1], residuals[3]),
    ]
    for level in range(2):
        for place in range(2):
            for to_c in range(8):
                at = 96 * place + 12 * to_c
                row = 24 * place + 12 * level
                pieces[to_c, row : row + 12] = solved[level][at : at + 12]
    pieces[:, 48:72] = solved[2].reshape(8, 24, 128)
    pieces[:, 72:96] = solved[3].reshape(8, 24, 128)
    lowest = solved[3]
    lowest_turned = turned(lowest)
    packs = shared[:, 96:128].reshape(256, 128)
    parts = (
        dot(shared[:, 32:64].reshape(256, 128), lowest[:128])
        + dot(shared[:, 64:96].reshape(256, 128), lowest_turned[:128])
        + dot(packs[:, :64], lowest[128:])
        + dot(packs[:, 64:], lowest_turned[128:])
    )
    pieces[:, 96:128] = parts.reshape(8, 32, 128)


def last_kernel(ranks, low, forward, inverse, basis, solved):
    back = cut(low[...], ranks[0, 0])
    rest = forward[...] - times_back(basis[0, 0, 0], basis[0, 0, 1], back)
    solved[0, 0] = times_back(inverse[0, 0, 0], inverse[0, 0, 1], rest)


def gather_kernel(parts, applied_keep, applied_got, lower_keep, lower_got, pieces):
    sums = []
    for place in range(2):
        total = jnp.zeros((8, 128), jnp.float32)
        for core in range(2):
            for at in range(8):
                total += parts[16 * core + 8 * place + at]
        sums.append(total)
    rows = [sums[place][row : row + 1] for row in range(3) for place in range(2)]
    rows += [sums[0][3:5] + sums[1][3:5]]
    tile = jnp.concatenate(rows, axis=0)
    for chip in range(16):
        pieces[chip, 0:8] = tile
        pieces[chip, 8:16] = lower_keep[chip] + lower_got[chip]
        pieces[chip, 16:80] = applied_keep[chip] + applied_got[chip]


def total_kernel(spots, parts, pieces, sums, lower):
    a = spots[0]
    tiles = []
    for at in range(4):
        total = parts[4 * at]
        for chip in range(1, 4):
            total += parts[4 * at + chip]
        tiles.append(total)
        lower[at] = total[8:16]
    upper = []
    for place in range(2):
        total = tiles[2 * place] + tiles[2 * place + 1]
        sums[place] = total[16:80]
        upper.append(total)
    rows = [tile[0:2] for tile in tiles]
    for start, stop in ((2, 4), (4, 6), (6, 7), (7, 8)):
        rows += [total[start:stop] for total in upper]
    rows += [jnp.zeros((4, 128), jnp.float32)]
    tile = jnp.concatenate(rows, axis=0)
    for place in range(32):
        pieces[place, 0:24] = tile
    everything = upper[0][16:64] + upper[1][16:64]
    for x in range(2):
        wide = jnp.where(a == 0, everything, upper[x][16:64])
        thin = upper[x][64:80]
        for at, slices in ((24, wide), (32, thin)):
            count = slices.shape[0] // 2
            gain = slices[count:]
            both = jnp.concatenate([slices[:count], gain], axis=-1)
            low = times_back(gain[:, :64], gain[:, 64:], both)
            for child in range(2):
                row = at + 4 * x + 2 * child
                pieces[:, row, :] = low[32 * child : 32 * child + 32, :128]
                pieces[:, row + 1, :] = low[32 * child : 32 * child + 32, 128:]


def forward_kernel(spots, ranks, gains, sums, lower, pieces, belows):
    a, d = spots[0], spots[3]
    coeffs3 = [cut(gains[:, at, :], ranks[6 + at]) for at in range(8)]
    pairs3 = [
        [jnp.concatenate([coeffs3[4 * x + y], coeffs3[4 * x + 2 + y]], axis=0) for y in range(2)]
        for x in range(2)
    ]

    def chain(total, gain, pair, limit):
        return cut(total - times(gain[:, :64], gain[:, 64:], pair), limit)

    pairs2 = []
    for x in range(2):
        both = [
            chain(
                gains[:, 8 + 2 * x + y, :],
                gains[:, 12 + 2 * x + y, :],
                pairs3[x][y],
                ranks[2 + 2 * x + y],
            )
            for y in range(2)
        ]
        pairs2.append(jnp.concatenate(both, axis=0))
    pair1 = jnp.concatenate(
        [chain(gains[:, 16 + x, :], gains[:, 18 + x, :], pairs2[x], ranks[x]) for x in range(2)],
        axis=0,
    )
    belows[0] = pair1
    belows[1] = jnp.where(a == 0, pairs2[0], pairs2[1])
    belows[2] = jnp.where(
        a == 0,
        jnp.where(d == 0, pairs3[0][0], pairs3[0][1]),
        jnp.where(d == 0, pairs3[1][0], pairs3[1][1]),
    )
    everything = sums[0, 0:48] + sums[1, 0:48]
    wide, upper = [], []
    for x in range(2):
        below = jnp.where(a == 0, pair1, jnp.where(d == 0, pairs3[x][0], pairs3[x][1]))
        slices = jnp.where(a == 0, everything, sums[x, 0:48])
        gain = slices[24:48]
        wide.append(slices[0:24] - times(gain[:, :64], gain[:, 64:], below))
        gain = sums[x, 56:64]
        upper.append(sums[x, 48:56] - times(gain[:, :64], gain[:, 64:], pairs2[x]))
    totals = []
    for place in range(2):
        total = jnp.zeros((16, 128), jnp.float32)
        for core in range(2):
            for at in range(8):
                total += gains[16 * core + 8 * place + at, 24:40]
        totals.append(total)
    joined = totals[0] + totals[1]
    nothing = jnp.zeros((2, 128), jnp.float32)
    tail = jnp.zeros((4, 128), jnp.float32)
    for to_a in range(2):
        for to_e in range(2):
            row = 4 * to_a + 2 * to_e
            tile = jnp.concatenate(
                [
                    upper[to_a][0:6],
                    lower[2 * to_a + to_e][0:6],
                    jnp.where(a == 0, joined[2 * to_a : 2 * to_a + 2], totals[0][row : row + 2]),
                    jnp.where(a == 0, nothing, totals[1][row : row + 2]),
                    joined[8 + 4 * to_a : 12 + 4 * to_a],
                    tail,
                ],
                axis=0,
            )
            for chip in range(4):
                place = 8 * to_a + 4 * to_e + chip
                pieces[place, 0:24] = wide[to_a]
                pieces[place, 24:48] = tile


def arrange_kernel(parts, mine, pieces):
    for chip in range(8):
        mine[24 * chip : 24 * chip + 24] = parts[chip, 0:24]
        mine[192 + 24 * chip : 216 + 24 * chip] = parts[8 + chip, 0:24]
    tails = [parts[chip, 24:48] for chip in range(16)]
    mine[384:480] = jnp.concatenate([tail[0:6] for tail in tails], axis=0)
    mine[480:576] = jnp.concatenate([tail[6:12] for tail in tails], axis=0)
    sums = []
    for place in range(2):
        total = tails[8 * place]
        for chip in range(1, 8):
            total += tails[8 * place + chip]
        sums.append(total[12:20])
    upper = sums[0] + sums[1]
    tail = jnp.zeros((2, 128), jnp.float32)
    for to_d in range(2):
        row = 2 * to_d
        tile = jnp.concatenate(
            [sums[0][0:2], upper[4 + row : 6 + row], sums[1][row : row + 2], tail], axis=0
        )
        for core in range(2):
            for to_c in range(8):
                pieces[16 * core + 8 * to_d + to_c] = tile


def flipped(values):
    return jnp.swapaxes(values, -1, -2)


def call(kernel, shapes, scalars, arrays, flops, fetched=()):
    count = len(fetched)
    places = len(scalars[0]) if isinstance(scalars[0:1] and scalars[0], tuple) else 0
    before = len(scalars) + len(arrays)
    scalars = [*scalars[0], *scalars[1:]] if places else scalars

    def outer(*refs):
        if places:
            refs = (tuple(ref[0] for ref in refs[:places]),) + refs[places:]
        inputs, sources = refs[:before], refs[before : before + count]
        outputs = refs[before + count : before + count + len(shapes)]
        buffers = refs[before + count + len(shapes) :]
        if count:
            sems = buffers[-1]
            copies = [
                pltpu.make_async_copy(source, buffer, sems.at[at])
                for at, (source, buffer) in enumerate(zip(sources, buffers[:-1]))
            ]
            for copy in copies:
                copy.start()
            for copy in copies:
                copy.wait()
        kernel(*inputs, *outputs, *buffers[:count])

    scratch = [pltpu.VMEM(array.shape, array.dtype) for array in fetched]
    if count:
        scratch.append(pltpu.SemaphoreType.DMA((count,)))
    return pl.pallas_call(
        outer,
        out_shape=[jax.ShapeDtypeStruct(shape, jnp.float32) for shape in shapes],
        in_specs=[pl.BlockSpec(memory_space=pltpu.SMEM)] * len(scalars)
        + [pl.BlockSpec(memory_space=pltpu.VMEM)] * len(arrays)
        + [pl.BlockSpec(memory_space=pltpu.HBM)] * count,
        out_specs=[pl.BlockSpec(memory_space=pltpu.VMEM)] * len(shapes),
        scratch_shapes=scratch,
        compiler_params=pltpu.CompilerParams(vmem_limit_bytes=(60 if count else 24) * 2**20),
        cost_estimate=pl.CostEstimate(flops=flops, bytes_accessed=4 * 2**20, transcendentals=0),
    )(*scalars, *arrays, *fetched)


def select(array, position):
    return lax.dynamic_index_in_dim(array, position, 0, keepdims=False)


def body(
    inverse_root,
    inverse_upper,
    inverse_middle,
    inverse_lower,
    leaf_inverse,
    source_root,
    source_upper,
    source_middle,
    source_lower,
    leaf_source,
    update_root,
    update_upper,
    update_middle,
    leaf_update,
    slots_root,
    slots_upper,
    slots_middle,
    leaf_slots,
    basis_upper,
    basis_middle,
    basis_lower,
    leaf_basis,
    front_ranks,
    leaf_ranks,
):
    a, e, k, d = (lax.axis_index(name) for name in ("a", "e", "k", "d"))
    separator, width = source_root.shape[2:]
    rank = leaf_basis.shape[-1]
    spots = tuple(axis.astype(jnp.int32).reshape(1) for axis in (a, e, k, d))

    leaf_forward, packs = call(
        leaf_kernel,
        [leaf_source.shape[2:], (8, 128, width)],
        [leaf_ranks],
        [],
        10**9,
        [leaf_inverse, leaf_source, flipped(leaf_basis), flipped(leaf_update), leaf_slots],
    )
    shared = exchange(packs, ("c",))

    keep, send, lows = call(
        apply_kernel,
        [(16, 64, width), (16, 64, width), (4, rank, width)],
        [spots],
        [],
        4 * 10**9,
        [
            flipped(inverse_root),
            inverse_upper,
            flipped(inverse_middle),
            source_root,
            source_upper,
            source_middle,
            flipped(update_root),
            flipped(update_upper),
            flipped(update_middle),
            slots_root,
            slots_upper,
            slots_middle,
            flipped(basis_upper),
            flipped(basis_middle),
        ],
    )
    applied = (keep, partner(send, "k"))
    keep, send, rows = call(
        lower_kernel,
        [(16, 8, width), (16, 8, width), (rank, 8, width)],
        [spots],
        [],
        10**9,
        [shared, lows, inverse_lower, source_lower, flipped(basis_lower)],
    )
    lower = (keep, partner(send, "k"))

    parts = exchange(rows, PLANE)
    (pieces,) = call(gather_kernel, [(16, 80, width)], [], [parts, *applied, *lower], 10**7)
    parts = exchange(pieces, CHIPS)
    pieces, sums, lower_slices = call(
        total_kernel, [(32, 40, width), (2, 64, width), (4, 8, width)], [spots], [parts], 10**7
    )
    gains = exchange(pieces, PLANE)

    pieces, belows = call(
        forward_kernel,
        [(16, 48, width), (3, 2 * rank, width)],
        [spots, front_ranks],
        [gains, sums, lower_slices],
        10**8,
    )
    parts = exchange(pieces, CHIPS)
    mine, pieces = call(
        arrange_kernel, [(3 * separator, width), (32, 8, width)], [], [parts], 10**7
    )
    theirs = partner(mine, "k")
    low_rows = exchange(pieces, PLANE)

    (pieces,) = call(
        backward_kernel,
        [(8, 128, width)],
        [spots, front_ranks],
        [
            gains,
            belows,
            low_rows,
            mine,
            theirs,
            flipped(inverse_root),
            inverse_upper,
            flipped(inverse_middle),
            inverse_lower,
            flipped(basis_upper),
            flipped(basis_middle),
            flipped(basis_lower),
            shared,
        ],
        3 * 10**9,
    )
    total = exchange(pieces, ("c",)).sum(axis=0)
    tops = total[:48].reshape(2, 24, width)
    tops = select(tops, d) + partner(select(tops, 1 - d), "d")
    (leaf_solution,) = call(
        last_kernel,
        [leaf_source.shape],
        [leaf_ranks],
        [total[96:], leaf_forward, leaf_inverse, flipped(leaf_basis)],
        10**9,
    )
    return (
        tops[None, None, :12],
        tops[None, None, 12:],
        total[None, None, 48:72],
        total[None, None, 72:96],
        leaf_solution,
    )


def solution(mesh):
    fine = Mesh(mesh.devices.reshape(2, 2, 4, 2, 2, 8), ROW + COL)
    tile = (ROW, COL)
    in_specs = (
        [P(*tile, None, None, None)] * 5
        + [P(ROW, None, None, None)] * 4
        + [P(*tile, None, None)]
        + [P(ROW, None, None, None, None, None)] * 3
        + [P(*tile, None, None, None)]
        + [P(ROW, None, None, None)] * 3
        + [P(*tile, None)]
        + [P(COL, None, None, None, None)] * 3
        + [P(*tile, None, None, None), P(), P(*tile)]
    )
    return jax.shard_map(
        body,
        mesh=fine,
        in_specs=tuple(in_specs),
        out_specs=(P(*tile, None, None),) * 5,
        check_vma=False,
    )
```
